32 devices in a mesh: rows: 8 (over y, x, core), chan: 4 (over z).
Axes of the slice: x: 2, y: 2, z: 4, core: 2. Of those that a mesh axis runs over, the one named last changes fastest.
Arguments:
- features: bfloat16 [4, 8192, 256], P('chan', 'rows'), may hold values from -6 to 6
- indices: int32 [4, 8192], P('chan', 'rows'), may hold values from 0 to 16383
- img_width: int32 [4, 32], P('chan'), may hold values from 0 to 32, as said below
- img_start: int32 [4, 32], P('chan'), may hold values from 0 to 8192, as said below
- codebook: bfloat16 [16384, 256], P('chan'), may hold values from -6 to 6
- w_in: bfloat16 [256, 512], replicated, may hold values from -0.375 to 0.375
- b_in: float32 [512], replicated, may hold values from -1.8 to 1.8
- gn1_gain: float32 [512], replicated, may hold values from 0.5 to 1.5
- gn1_bias: float32 [512], replicated, may hold values from -1.8 to 1.8
- conv1_w: bfloat16 [3, 3, 512, 512], replicated, may hold values from -0.09375 to 0.09375
- conv1_b: float32 [512], replicated, may hold values from -1.8 to 1.8
- gn2_gain: float32 [512], replicated, may hold values from 0.5 to 1.5
- gn2_bias: float32 [512], replicated, may hold values from -1.8 to 1.8
- conv2_w: bfloat16 [3, 3, 512, 512], replicated, may hold values from -0.1875 to 0.1875
- conv2_b: float32 [512], replicated, may hold values from -1.8 to 1.8
- gn3_gain: float32 [512], replicated, may hold values from 0.5 to 1.5
- gn3_bias: float32 [512], replicated, may hold values from -1.8 to 1.8
- w_query: bfloat16 [512, 512], replicated, may hold values from -0.5 to 0.5
- b_query: float32 [512], replicated, may hold values from -1.8 to 1.8
- w_key: bfloat16 [512, 512], replicated, may hold values from -0.25 to 0.25
- w_value: bfloat16 [512, 512], replicated, may hold values from -0.25 to 0.25
- b_value: float32 [512], replicated, may hold values from -1.8 to 1.8
- w_proj: bfloat16 [512, 512], replicated, may hold values from -3 to 3
- b_proj: float32 [512], replicated, may hold values from -1.8 to 1.8
- cotangent: bfloat16 [4, 8192, 512], P('chan', 'rows'), may hold values from -6 to 6
Outputs:
- output: bfloat16 [4, 8192, 512], P('chan', 'rows')
- feature_grad: bfloat16 [4, 8192, 256], P('chan', 'rows')
- codebook_grad: float32 [16384, 256], P('chan')
- grad_w_in: float32 [256, 512], replicated
- grad_b_in: float32 [512], replicated
- grad_gn1_gain: float32 [512], replicated
- grad_gn1_bias: float32 [512], replicated
- grad_conv1_w: float32 [3, 3, 512, 512], replicated
- grad_conv1_b: float32 [512], replicated
- grad_gn2_gain: float32 [512], replicated
- grad_gn2_bias: float32 [512], replicated
- grad_conv2_w: float32 [3, 3, 512, 512], replicated
- grad_conv2_b: float32 [512], replicated
- grad_gn3_gain: float32 [512], replicated
- grad_gn3_bias: float32 [512], replicated
- grad_w_query: float32 [512, 512], replicated
- grad_b_query: float32 [512], replicated
- grad_w_key: float32 [512, 512], replicated
- grad_w_value: float32 [512, 512], replicated
- grad_b_value: float32 [512], replicated
- grad_w_proj: float32 [512, 512], replicated
- grad_b_proj: float32 [512], replicated
The draws below stay inside these ranges and needn't reach their ends.
Inputs may be any that keep to these rules, and one draw needn't show every extreme that they name: `img_width`: each group's images in slot order have sides half of 32, three quarters of 32 or 32; the first has three quarters of 32, the second 32; slots after the last image hold 0. `img_start`: images follow one another without gaps from pixel 0 and fill the group's 8192 pixels; no image but the last ends at a multiple of 1024 pixels; unused slots hold 8192.
All inputs are finite; a program needn't handle non-finite values.
Results may differ from the reference program's by a relative error of at most 0.02.
Values may be sent and summed in bfloat16 or wider, within the bound.
No kernel may reach another device: no remote copies, remote signals or barrier semaphores. Data moves between devices by JAX's collectives and lax.ppermute only.
A program may use at most 256 MiB of HBM per device.

```python
import math
import jax
import jax.numpy as jnp
from jax import lax

C = 512
EMB = 256
K = 16384
GN_GROUPS = 32
PIX_DEV = 1024
GRID = 32
QBLOCK = 512
GROUPS = 4
GPIX = 8192
NIMG = 32


small_sums = (0, 4, 8, 9, 12, 13, 16, 17, 18, 20, 21, 22)


def representable(amount):
    listed = jnp.array(small_sums, dtype=jnp.int32)
    return (amount >= 24) | jnp.any(amount == listed)


def image_tables(key):
    unit_px = GRID // 4 * (GRID // 4)
    total_units = GPIX // unit_px
    band_units = PIX_DEV // unit_px
    unit_sizes = jnp.array([4, 9, 16], dtype=jnp.int32)
    side_sizes = jnp.array([GRID // 2, 3 * GRID // 4, GRID], dtype=jnp.int32)
    forced = jnp.array([9, 16], dtype=jnp.int32)

    def one_group(group_key):

        def place(used_units, slot):
            remain = total_units - used_units
            after_use = used_units + unit_sizes
            allowed = (unit_sizes <= remain) & jax.vmap(representable)(remain - unit_sizes)
            allowed = allowed & ((after_use % band_units != 0) | (after_use == total_units))
            wanted = forced[jnp.minimum(slot, 1)]
            allowed = allowed & ((slot >= 2) | (unit_sizes == wanted))
            valid_count = jnp.sum(allowed.astype(jnp.int32))
            pick_at = jax.random.randint(jax.random.fold_in(group_key, slot), (), 0, jnp.maximum(valid_count, 1))
            rank_of = jnp.cumsum(allowed.astype(jnp.int32)) - 1
            chosen = allowed & (rank_of == pick_at)
            which_one = jnp.sum(chosen.astype(jnp.int32) * jnp.arange(3, dtype=jnp.int32))
            active = remain > 0
            side_px = jnp.where(active, side_sizes[which_one], 0)
            begin_at = jnp.where(active, used_units * unit_px, GPIX)
            used_units = used_units + jnp.where(active, unit_sizes[which_one], 0)
            return (used_units, (side_px.astype(jnp.int32), begin_at.astype(jnp.int32)))
        final_used, tables = lax.scan(place, jnp.int32(0), jnp.arange(NIMG, dtype=jnp.int32))
        return tables
    group_keys = jax.vmap(lambda group_index: jax.random.fold_in(key, group_index))(jnp.arange(GROUPS, dtype=jnp.int32))
    return jax.vmap(one_group)(group_keys)


def draw_img_width(key, part):
    return image_tables(jax.random.fold_in(key, 11))[0]


def draw_img_start(key, part):
    return image_tables(jax.random.fold_in(key, 11))[1]


def with_ends(values, key, least, largest):
    spot = [jax.random.randint(jax.random.fold_in(key, axis), (), 0, length) for axis, length in enumerate(values.shape)]
    widest = values.shape.index(max(values.shape))
    next_to = spot[:widest] + [(spot[widest] + 1) % values.shape[widest]] + spot[widest + 1:]
    return values.at[tuple(spot)].set(least).at[tuple(next_to)].set(largest)


def level_of(key, shape, split, least, largest):
    loudness = 1.0
    for axis_at, parts in split:
        heights = jax.random.uniform(jax.random.fold_in(jax.random.fold_in(key, 6), axis_at), (parts,), jnp.float32, least / len(split), largest / len(split))
        loudness = loudness * jnp.repeat(jnp.exp(heights), shape[axis_at] // parts).reshape((-1,) + (1,) * (len(shape) - 1 - axis_at))
    return loudness


def gaussian(key, shape, scale, reach, split=(), held_as=jnp.bfloat16):
    entries = jax.random.normal(key, shape, jnp.float32) * scale
    if len(split) > 0:
        entries = level_of(key, shape, split, -0.22, 0.18) * entries
    return jnp.clip(entries, min=-reach, max=reach).astype(held_as)


def setup_inputs(seed: int = 0) -> dict:
    key_list = jax.random.split(jax.random.key(seed), 26)
    features = gaussian(key_list[0], (GROUPS, GPIX, EMB), 1.0, 6.0, ((0, 4), (1, 8)))
    indices = with_ends(jax.random.randint(key_list[1], (GROUPS, GPIX), 0, K), jax.random.fold_in(key_list[1], 1), 0, K - 1).astype(jnp.int32)
    img_width = draw_img_width(jax.random.fold_in(key_list[25], 71), 0)
    img_start = draw_img_start(jax.random.fold_in(key_list[25], 71), 0)
    codebook = gaussian(key_list[4], (K, EMB), 1.0, 6.0, ((0, 4),))
    w_in = gaussian(key_list[5], (EMB, C), EMB ** -0.5, 0.375)
    b_in = gaussian(key_list[6], (C,), 0.3, 1.8, (), jnp.float32)
    gn1_gain = jnp.clip(1.0 + 0.1 * jax.random.normal(key_list[7], (C,), jnp.float32), 0.5, 1.5)
    gn1_bias = gaussian(key_list[8], (C,), 0.3, 1.8, (), jnp.float32)
    conv1_w = gaussian(key_list[9], (3, 3, C, C), (9 * C) ** -0.5, 0.09375)
    conv1_b = gaussian(key_list[10], (C,), 0.3, 1.8, (), jnp.float32)
    gn2_gain = jnp.clip(1.0 + 0.1 * jax.random.normal(key_list[11], (C,), jnp.float32), 0.5, 1.5)
    gn2_bias = gaussian(key_list[12], (C,), 0.3, 1.8, (), jnp.float32)
    conv2_w = gaussian(key_list[13], (3, 3, C, C), (9 * C // 4) ** -0.5, 0.1875)
    conv2_b = gaussian(key_list[14], (C,), 0.3, 1.8, (), jnp.float32)
    gn3_gain = jnp.clip(1.0 + 0.1 * jax.random.normal(key_list[15], (C,), jnp.float32), 0.5, 1.5)
    gn3_bias = gaussian(key_list[16], (C,), 0.3, 1.8, (), jnp.float32)
    w_query = gaussian(key_list[17], (C, C), (C // 4) ** -0.5, 0.5)
    b_query = gaussian(key_list[18], (C,), 0.3, 1.8, (), jnp.float32)
    w_key = gaussian(key_list[19], (C, C), C ** -0.5, 0.25)
    w_value = gaussian(key_list[20], (C, C), C ** -0.5, 0.25)
    b_value = gaussian(key_list[21], (C,), 0.3, 1.8, (), jnp.float32)
    w_proj = gaussian(key_list[22], (C, C), (max(C // 128, 1)) ** -0.5, 3.0)
    b_proj = gaussian(key_list[23], (C,), 0.3, 1.8, (), jnp.float32)
    cotangent = gaussian(key_list[24], (GROUPS, GPIX, C), 1.0, 6.0, ((0, 4), (1, 8)))
    return dict(features=features, indices=indices, img_width=img_width, img_start=img_start, codebook=codebook, w_in=w_in, b_in=b_in, gn1_gain=gn1_gain, gn1_bias=gn1_bias, conv1_w=conv1_w, conv1_b=conv1_b, gn2_gain=gn2_gain, gn2_bias=gn2_bias, conv2_w=conv2_w, conv2_b=conv2_b, gn3_gain=gn3_gain, gn3_bias=gn3_bias, w_query=w_query, b_query=b_query, w_key=w_key, w_value=w_value, b_value=b_value, w_proj=w_proj, b_proj=b_proj, cotangent=cotangent)


@jax.custom_vjp
def low(v):
    return lax.optimization_barrier(v.astype(jnp.bfloat16)).astype(jnp.float32)

@jax.custom_vjp
def low_back(v):
    return v

def low_keep(v):
    return (low(v), None)

def low_pass(kept, grad):
    return (grad,)

def back_keep(v):
    return (v, None)

def back_low(kept, grad):
    return (low(grad),)
low.defvjp(low_keep, low_pass)
low_back.defvjp(back_keep, back_low)
highest = lax.Precision.HIGHEST
epsilon = 1e-06
masked_score = -1e+30

def layout(positions, widths, starts, stream_len):
    before = (starts[None, :] <= positions[:, None]).astype(jnp.int32)
    image_id = lax.optimization_barrier(jnp.sum(before, axis=1)) - 1
    inside = (positions >= 0) & (positions < stream_len)
    image_id = jnp.where(inside, image_id, -1)
    slot_ids = jnp.arange(widths.shape[0], dtype=jnp.int32)
    choose = (image_id[:, None] == slot_ids[None, :]).astype(jnp.int32)
    side_len = lax.optimization_barrier(jnp.sum(choose * widths[None, :], axis=1))
    begin_at = lax.optimization_barrier(jnp.sum(choose * starts[None, :], axis=1))
    offset = positions - begin_at
    safe_side = jnp.maximum(side_len, 1)
    return (image_id, side_len, offset // safe_side, offset % safe_side)

def tap_table(side_len, row_at, col_at, rim_len):
    pixel_count = side_len.shape[0]
    centre = jnp.arange(pixel_count, dtype=jnp.int32) + rim_len
    index_list = []
    valid_list = []
    for delta_r in (-1, 0, 1):
        for delta_c in (-1, 0, 1):
            index_list.append(centre + delta_r * side_len + delta_c)
            valid_list.append((row_at + delta_r >= 0) & (row_at + delta_r < side_len) & (col_at + delta_c >= 0) & (col_at + delta_c < side_len))
    return (jnp.stack(index_list, axis=1), jnp.stack(valid_list, axis=1))

def conv_apply(values, weight, tap_index, tap_valid, rim_len):
    extended = jnp.pad(values, ((rim_len, rim_len), (0, 0)))
    picked = jnp.take(extended, tap_index, axis=0)
    picked = jnp.where(tap_valid[:, :, None], picked, 0.0)
    flat_rows = picked.reshape(tap_index.shape[0], -1)
    return jnp.dot(flat_rows, weight.reshape(-1, weight.shape[3]), precision=highest)

def group_norm(values, image_id, widths, gain, bias):
    slots = widths.shape[0]
    channels = values.shape[1]
    per_group = channels // GN_GROUPS
    counts = (jnp.maximum(widths * widths, 1) * per_group).astype(jnp.float32)
    first_sum = jax.ops.segment_sum(values, image_id, num_segments=slots).reshape(slots, GN_GROUPS, per_group).sum(axis=2)
    second_sum = jax.ops.segment_sum(values * values, image_id, num_segments=slots).reshape(slots, GN_GROUPS, per_group).sum(axis=2)
    mean_val = first_sum / counts[:, None]
    variance = second_sum / counts[:, None] - mean_val * mean_val
    inv_std = lax.rsqrt(variance + epsilon)
    mean_full = jnp.repeat(jnp.take(mean_val, image_id, axis=0), per_group, axis=1)
    inv_full = jnp.repeat(jnp.take(inv_std, image_id, axis=0), per_group, axis=1)
    return (values - mean_full) * inv_full * gain + bias

def swish_act(values):
    return values * jax.nn.sigmoid(values)

def attention(query_rows, key_rows, value_rows, image_id, key_ids, key_rim):
    pixel_count = query_rows.shape[0]
    chans = query_rows.shape[1]
    window = QBLOCK + 2 * key_rim
    score_scale = 1.0 / math.sqrt(chans)
    kv_ext = jnp.pad(jnp.concatenate([key_rows, value_rows], axis=1), ((key_rim, key_rim), (0, 0)))

    def block_out(block_at):
        query_blk = lax.dynamic_slice_in_dim(query_rows, block_at, QBLOCK)
        kv_blk = lax.dynamic_slice_in_dim(kv_ext, block_at, window)
        key_blk = kv_blk[:, :chans]
        value_blk = kv_blk[:, chans:]
        id_query = lax.dynamic_slice_in_dim(image_id, block_at, QBLOCK)
        id_key = lax.dynamic_slice_in_dim(key_ids, block_at, window)
        scores = low_back(jnp.dot(query_blk, key_blk.T, precision=highest) * score_scale)
        keep_mask = (id_query[:, None] == id_key[None, :]) & (id_key[None, :] >= 0)
        scores = jnp.where(keep_mask, scores, masked_score)
        row_max = lax.optimization_barrier(jnp.max(scores, axis=1, keepdims=True))
        exp_val = jnp.exp(scores - row_max)
        prob_rows = exp_val / lax.optimization_barrier(jnp.sum(exp_val, axis=1, keepdims=True))
        return jnp.dot(low(prob_rows), value_blk, precision=highest)
    block_starts = jnp.arange(pixel_count // QBLOCK, dtype=jnp.int32) * QBLOCK
    mixed_rows = lax.map(jax.checkpoint(block_out), block_starts)
    return mixed_rows.reshape(pixel_count, chans)

def group_forward(params, code_book, feature_rows, code_index, widths, starts):
    w_in, b_in, gn1_gain, gn1_bias, conv1_w, conv1_b, gn2_gain, gn2_bias, conv2_w, conv2_b, gn3_gain, gn3_bias, w_query, b_query, w_key, w_value, b_value, w_proj, b_proj = params
    stream_len = feature_rows.shape[0]
    conv_rim = 2 * GRID
    key_rim = GRID * GRID
    positions = jnp.arange(stream_len, dtype=jnp.int32)
    image_id, side_len, row_at, col_at = layout(positions, widths, starts, stream_len)
    key_pos = jnp.arange(stream_len + 2 * key_rim, dtype=jnp.int32) - key_rim
    key_ids = layout(key_pos, widths, starts, stream_len)[0]
    tap_index, tap_valid = tap_table(side_len, row_at, col_at, conv_rim)
    quant_rows = low_back(low(feature_rows + jnp.take(code_book, code_index, axis=0)))
    resid_in = low_back(jnp.dot(quant_rows, w_in, precision=highest) + b_in)
    act_one = low(swish_act(group_norm(resid_in, image_id, widths, gn1_gain, gn1_bias)))
    hid_one = low_back(conv_apply(act_one, conv1_w, tap_index, tap_valid, conv_rim) + conv1_b)
    act_two = low(swish_act(group_norm(hid_one, image_id, widths, gn2_gain, gn2_bias)))
    hid_two = low_back(conv_apply(act_two, conv2_w, tap_index, tap_valid, conv_rim) + conv2_b)
    resid_mid = resid_in + hid_two
    normed = low(group_norm(resid_mid, image_id, widths, gn3_gain, gn3_bias))
    query_rows = low_back(low(jnp.dot(normed, w_query, precision=highest) + b_query))
    key_rows = low_back(low(jnp.dot(normed, w_key, precision=highest)))
    value_rows = low_back(low(jnp.dot(normed, w_value, precision=highest) + b_value))
    attn_rows = low_back(low(attention(query_rows, key_rows, value_rows, image_id, key_ids, key_rim)))
    return resid_mid + jnp.dot(attn_rows, w_proj, precision=highest) + b_proj

def reference(features, indices, img_width, img_start, codebook, w_in, b_in, gn1_gain, gn1_bias, conv1_w, conv1_b, gn2_gain, gn2_bias, conv2_w, conv2_b, gn3_gain, gn3_bias, w_query, b_query, w_key, w_value, b_value, w_proj, b_proj, cotangent):
    params = tuple((weight_arr.astype(jnp.float32) for weight_arr in (w_in, b_in, gn1_gain, gn1_bias, conv1_w, conv1_b, gn2_gain, gn2_bias, conv2_w, conv2_b, gn3_gain, gn3_bias, w_query, b_query, w_key, w_value, b_value, w_proj, b_proj)))
    code_book = codebook.astype(jnp.float32)

    def one_group(totals, item):
        feature_rows, code_index, widths, starts, cot_rows = item

        def forward(weights, book_arr, rows_arr):
            return group_forward(weights, book_arr, rows_arr, code_index, widths, starts)
        result, pullback = jax.vjp(forward, params, code_book, feature_rows.astype(jnp.float32))
        grad_w, grad_book, grad_rows = pullback(cot_rows.astype(jnp.float32))
        totals = jax.tree.map(jnp.add, totals, (grad_w, grad_book))
        return (totals, (result.astype(jnp.bfloat16), grad_rows.astype(jnp.bfloat16)))
    zeros_init = jax.tree.map(jnp.zeros_like, (params, code_book))
    (grad_w, grad_book), (output, feature_grad) = lax.scan(one_group, zeros_init, (features, indices, img_width, img_start, cotangent))
    return (output, feature_grad, grad_book, grad_w[0], grad_w[1], grad_w[2], grad_w[3], grad_w[4], grad_w[5], grad_w[6], grad_w[7], grad_w[8], grad_w[9], grad_w[10], grad_w[11], grad_w[12], grad_w[13], grad_w[14], grad_w[15], grad_w[16], grad_w[17], grad_w[18])
```

```python
import functools
import math

import jax
import jax.numpy as jnp
from jax import lax
from jax.experimental import pallas as pl
from jax.experimental.pallas import tpu as pltpu
from jax.sharding import PartitionSpec as P

GN_GROUPS = 32
GRID = 32
BLK = (GRID // 4) ** 2
HALO = 64
CHUNK = 256
STAT = 16
epsilon = 1e-06
masked_score = -1e30
f32 = jnp.float32
bf16 = jnp.bfloat16
MIB = 1 << 20
LATE_ROUND = 2
BOOK_ROUND = 4

VM = pl.BlockSpec(memory_space=pltpu.VMEM)
SM = pl.BlockSpec(memory_space=pltpu.SMEM)
HB = pl.BlockSpec(memory_space=pl.ANY)


def call(body, ins, outs, scratch, operands, flops, vmem=58, aliases={}, light=False):
    bytes_all = sum(math.prod(a.shape) * a.dtype.itemsize for a in (*operands, *[o[0] for o in outs]))
    if light:
        flops = bytes_all = 0
    return pl.pallas_call(
        body,
        out_shape=[o[0] for o in outs],
        in_specs=ins,
        out_specs=[o[1] for o in outs],
        scratch_shapes=scratch,
        input_output_aliases=aliases,
        compiler_params=pltpu.CompilerParams(vmem_limit_bytes=vmem * MIB),
        cost_estimate=pl.CostEstimate(flops=flops, bytes_accessed=bytes_all, transcendentals=0),
    )(*operands)


def sds(shape, dtype):
    return jax.ShapeDtypeStruct(shape, dtype)


def dot_nn(a, b):
    return lax.dot_general(a, b, (((1,), (0,)), ((), ())), preferred_element_type=f32)


def dot_nt(a, b):
    return lax.dot_general(a, b, (((1,), (1,)), ((), ())), preferred_element_type=f32)


def dot_tn(a, b):
    return lax.dot_general(a, b, (((0,), (0,)), ((), ())), preferred_element_type=f32)


def group_total(x):
    per = x.shape[1] // GN_GROUPS
    lane = lax.broadcasted_iota(jnp.int32, x.shape, 1)
    step = 1
    while step < per:
        up = pltpu.roll(x, step, 1)
        down = pltpu.roll(x, x.shape[1] - step, 1)
        x = x + jnp.where((lane & step) != 0, up, down)
        step *= 2
    return x


def image_total(e_ref, row, nb, amat):
    total = amat[:, 0:1] * e_ref[row : row + 1, :]
    for j in range(1, nb):
        total = total + amat[:, j : j + 1] * e_ref[row + j : row + j + 1, :]
    return total


def split3(v):
    high = v.astype(bf16)
    rest = v - high.astype(f32)
    mid = rest.astype(bf16)
    low = (rest - mid.astype(f32)).astype(bf16)
    return high, mid, low


def pack_stats(a, b):
    rows = [p.astype(f32) for p in (*split3(a), *split3(b))]
    rows.append(jnp.zeros((STAT - 6, a.shape[1]), f32))
    return jnp.concatenate(rows, axis=0).astype(bf16)


def unpack_stats(block):
    v = block.astype(f32)
    return v[0:1] + v[1:2] + v[2:3], v[3:4] + v[4:5] + v[5:6]


def stat_rows(a, b):
    return jnp.concatenate([a, b, jnp.zeros((6, a.shape[1]), f32)], axis=0)


def totals(t_ref, nb, amat, prev_rows, next_rows):
    first, last = amat[:, nb : nb + 1], amat[:, nb + 1 : nb + 2]
    one = t_ref[0:nb, :] + first * prev_rows[0] + last * next_rows[0]
    two = t_ref[nb : 2 * nb, :] + first * prev_rows[1] + last * next_rows[1]
    inv_count = amat[:, nb + 2 : nb + 3]
    return one * inv_count, two * inv_count


def norm_stats(t_ref, nb, amat, prev_rows, next_rows, stat_ref):
    mean, square = totals(t_ref, nb, amat, prev_rows, next_rows)
    stat_ref[0:nb, :] = mean
    stat_ref[nb : 2 * nb, :] = lax.rsqrt(square - mean * mean + epsilon)


def block_stats(stat_ref, nb, k):
    return stat_ref[k : k + 1, :], stat_ref[nb + k : nb + k + 1, :]


def own_totals(e_ref, nb, amat, t_ref):
    t_ref[0:nb, :] = group_total(image_total(e_ref, 0, nb, amat))
    t_ref[nb : 2 * nb, :] = group_total(image_total(e_ref, nb, nb, amat))


def set_sums(e_ref, nb, k, x, y):
    e_ref[k : k + 1, :] = jnp.sum(x, axis=0, keepdims=True)
    e_ref[nb + k : nb + k + 1, :] = jnp.sum(y, axis=0, keepdims=True)


def silu(pre):
    return pre * jax.nn.sigmoid(pre)


def silu_slope(pre):
    s = jax.nn.sigmoid(pre)
    return s * (1.0 + pre * (1.0 - s))


def shift_columns(mid_ref, left_ref, right_ref, rows):
    left_ref[8 : 8 + rows, :] = mid_ref[7 : 7 + rows, :]
    right_ref[8 : 8 + rows, :] = mid_ref[9 : 9 + rows, :]


def make_patch(refs, patch_ref, mask_ref, ints_ref, k, chans):
    side = ints_ref[0, k]
    for dr in (-1, 0, 1):
        at = 8 + HALO + k * BLK
        if dr != 0:
            at = pl.multiple_of(at + dr * side, 8)
        for dc in (-1, 0, 1):
            tap = (dr + 1) * 3 + dc + 1
            rows = refs[dc + 1][pl.ds(at, BLK), :]
            if tap != 4:
                rows = rows * mask_ref[k * BLK : (k + 1) * BLK, tap : tap + 1]
            patch_ref[k * BLK : (k + 1) * BLK, tap * chans : (tap + 1) * chans] = rows.astype(bf16)


def lookup_kernel(tokens, *refs):
    index_ref, book_ref, out_ref = refs[tokens:]
    codes = book_ref.shape[0]
    total = jnp.zeros(out_ref.shape, f32)
    for c in range(0, codes, 512):
        lane = lax.broadcasted_iota(jnp.int32, (index_ref.shape[0], 512), 1) + c
        hot = jnp.where(index_ref[...] == lane, 1.0, 0.0).astype(bf16)
        total = total + dot_nn(hot, book_ref[c : c + 512, :])
    out_ref[...] = total.astype(bf16)


def lookup(index, book, tokens=()):
    pixels, emb = index.shape[0], book.shape[1]
    step = 256
    return pl.pallas_call(
        functools.partial(lookup_kernel, len(tokens)),
        grid=(pixels // step,),
        out_shape=sds((pixels, emb), bf16),
        in_specs=[HB] * len(tokens) + [pl.BlockSpec((step, 1), lambda i: (i, 0)), pl.BlockSpec(book.shape, lambda i: (0, 0))],
        out_specs=pl.BlockSpec((step, emb), lambda i: (i, 0)),
        compiler_params=pltpu.CompilerParams(vmem_limit_bytes=40 * MIB),
        cost_estimate=pl.CostEstimate(
            flops=2 * pixels * book.shape[0] * emb, bytes_accessed=book.size * 2, transcendentals=0
        ),
    )(*tokens, index, book)


def scatter_kernel(step, tokens, parts, *refs):
    index_refs, grad_refs = refs[tokens : tokens + parts], refs[tokens + parts : tokens + 3 * parts]
    begun_ref, out_ref = refs[-2:]
    half, emb = step * pl.num_programs(0), grad_refs[0].shape[1]
    for side in range(2):
        lanes = slice(side * emb, (side + 1) * emb)
        code = lax.broadcasted_iota(jnp.int32, (step, 512), 0) + (pl.program_id(0) * step + side * half)
        total = begun_ref[:, lanes]
        for index_ref, one_ref, two_ref in zip(index_refs, grad_refs[::2], grad_refs[1::2]):
            for p in range(0, one_ref.shape[0], 512):
                hot = jnp.where(index_ref[0:1, p : p + 512] == code, 1.0, 0.0).astype(bf16)
                grad = one_ref[p : p + 512, :].astype(f32) + two_ref[p : p + 512, :].astype(f32)
                total = total + dot_nn(hot, grad.astype(bf16))
        out_ref[:, lanes] = total.astype(out_ref.dtype)


def scatter(indices, pairs, codes, dtype, begun, tokens):
    grads = [x for pair in pairs for x in pair]
    emb, step, parts = grads[0].shape[1], 256, len(pairs)
    whole = [pl.BlockSpec(a.shape, lambda i: (0, 0)) for a in (*indices, *grads)]
    tile = pl.BlockSpec((step, 2 * emb), lambda i: (i, 0))
    return pl.pallas_call(
        functools.partial(scatter_kernel, step, len(tokens), parts),
        grid=(codes // 2 // step,),
        out_shape=sds((codes // 2, 2 * emb), dtype),
        in_specs=[HB for _ in tokens] + whole + [tile],
        out_specs=tile,
        compiler_params=pltpu.CompilerParams(vmem_limit_bytes=40 * MIB),
        cost_estimate=pl.CostEstimate(
            flops=2 * parts * grads[0].shape[0] * codes * emb, bytes_accessed=codes * emb * 8, transcendentals=0
        ),
    )(*tokens, *indices, *grads, begun)


def own_kernel(step, pass_ref, token_ref, index_ref, grad_ref, quant_ref, err_ref, in_ref, one_ref, two_ref, three_ref,
               query_ref, value_ref, proj_ref, passed_ref, out_ref, small_ref):
    emb = grad_ref.shape[1]
    half = out_ref.shape[0]
    for r in range(0, half, step):
        for side in range(2):
            code = lax.broadcasted_iota(jnp.int32, (step, 512), 0) + (r + side * half)
            total = jnp.zeros((step, emb), f32)
            for p in range(0, grad_ref.shape[0], 512):
                hot = jnp.where(index_ref[0:1, p : p + 512] == code, 1.0, 0.0).astype(bf16)
                total = total + dot_nn(hot, grad_ref[p : p + 512, :])
            out_ref[r : r + step, side * emb : (side + 1) * emb] = total
    small_ref[0:emb, :] = dot_tn(quant_ref[...], err_ref[...]).astype(bf16)
    rows = [in_ref[0:1, :], one_ref[0:3, :], two_ref[0:3, :], three_ref[0:2, :], query_ref[...], value_ref[...], proj_ref[...]]
    filler = jnp.zeros((small_ref.shape[0] - emb - 12, small_ref.shape[1]), f32)
    small_ref[emb:, :] = jnp.concatenate([*rows, filler], axis=0).astype(bf16)


def own_part(passed, token, index, grad, quant, err, vectors, codes):
    emb, chans = grad.shape[1], err.shape[1]
    outs = [(sds(passed.shape, bf16), HB), (sds((codes // 2, 2 * emb), f32), VM), (sds((chans, chans), bf16), VM)]
    operands = (passed, token, index, grad, quant, err, *vectors)
    flops = 2 * grad.shape[0] * emb * (codes + chans)
    return call(functools.partial(own_kernel, 256), [HB] * 2 + [VM] * (len(operands) - 2), outs, [], operands, flops, aliases={0: 0})


def lift_kernel(n_codes, nb, *refs):
    feat_ref, code_refs = refs[0], refs[1 : 1 + n_codes]
    w_ref, b_ref, amat_ref, quant_ref, resid_ref, t_ref, msgp_ref, msgn_ref, e_ref = refs[1 + n_codes :]
    pixels = feat_ref.shape[0]
    for c in range(0, pixels, CHUNK):
        at = slice(c, c + CHUNK)
        code = code_refs[0][at, :].astype(f32)
        for other in code_refs[1:]:
            code = code + other[at, :].astype(f32)
        quant = (feat_ref[at, :].astype(f32) + code).astype(bf16)
        quant_ref[at, :] = quant
        resid_ref[at, :] = dot_nn(quant, w_ref[...]) + b_ref[...]
    for k in range(nb):
        x = resid_ref[k * BLK : (k + 1) * BLK, :]
        set_sums(e_ref, nb, k, x, x * x)
    own_totals(e_ref, nb, amat_ref[...], t_ref)
    send_rows(resid_ref, t_ref, nb, msgp_ref, msgn_ref)


def send_rows(x_ref, t_ref, nb, msgp_ref, msgn_ref):
    pixels = x_ref.shape[0]
    msgp_ref[0:HALO, :] = x_ref[0:HALO, :]
    msgn_ref[0:HALO, :] = x_ref[pixels - HALO : pixels, :]
    send_stats(t_ref, nb, msgp_ref, msgn_ref, HALO)


def send_stats(t_ref, nb, msgp_ref, msgn_ref, at):
    msgp_ref[at : at + 8, :] = stat_rows(t_ref[0:1, :], t_ref[nb : nb + 1, :])
    msgn_ref[at : at + 8, :] = stat_rows(t_ref[nb - 1 : nb, :], t_ref[2 * nb - 1 : 2 * nb, :])


def get_stats(ref, at):
    return ref[at : at + 1, :], ref[at + 1 : at + 2, :]


def conv_forward_kernel(nb, last, *refs):
    x_ref, rp_ref, rn_ref, t_ref, amat_ref, gain_ref, bias_ref, mask_ref, ints_ref, w_hbm, cb_ref = refs[:11]
    refs = refs[11:]
    if last:
        resid_ref, cot_ref = refs[:2]
        refs = refs[2:]
    out_ref, stat_ref, to_ref, msgp_ref, msgn_ref, patch_hbm = refs[:6]
    mid_ref, left_ref, right_ref, patch_ref, w_ref, e_ref, w_sem, p_sem = refs[6:]
    pixels, chans = x_ref.shape
    load = pltpu.make_async_copy(w_hbm, w_ref, w_sem)
    load.start()
    amat = amat_ref[...]
    norm_stats(t_ref, nb, amat, get_stats(rp_ref, HALO), get_stats(rn_ref, HALO), stat_ref)
    gain, bias = gain_ref[...], bias_ref[...]

    def act(x, k):
        mean, inv = block_stats(stat_ref, nb, k)
        return silu((x - mean) * (inv * gain) + bias).astype(bf16).astype(f32)

    mid_ref[8 : 8 + HALO, :] = act(rp_ref[0:HALO, :], 0)
    mid_ref[8 + HALO + pixels : 8 + 2 * HALO + pixels, :] = act(rn_ref[0:HALO, :], nb - 1)
    for k in range(nb):
        mid_ref[8 + HALO + k * BLK : 8 + HALO + (k + 1) * BLK, :] = act(x_ref[k * BLK : (k + 1) * BLK, :], k)
    shift_columns(mid_ref, left_ref, right_ref, pixels + 2 * HALO)
    saves = []
    for c in range(0, pixels, CHUNK):
        for k in range(c // BLK, (c + CHUNK) // BLK):
            make_patch((left_ref, mid_ref, right_ref), patch_ref, mask_ref, ints_ref, k, chans)
        save = pltpu.make_async_copy(
            patch_ref.at[pl.ds(c, CHUNK), :], patch_hbm.at[pl.ds(c, CHUNK), :], p_sem.at[c // CHUNK]
        )
        save.start()
        saves.append(save)
        if c == 0:
            load.wait()
        out = dot_nn(patch_ref[c : c + CHUNK, :], w_ref[...]) + cb_ref[...]
        if last:
            out = out + resid_ref[c : c + CHUNK, :]
        out_ref[c : c + CHUNK, :] = out
        for k in range(c // BLK, (c + CHUNK) // BLK):
            x = out_ref[k * BLK : (k + 1) * BLK, :]
            set_sums(e_ref, nb, k, x, x * x)
    own_totals(e_ref, nb, amat, to_ref)
    if last:
        msgp_ref[0:pixels, :] = out_ref[...].astype(bf16)
        msgn_ref[0:pixels, :] = out_ref[...].astype(bf16)
        msgp_ref[pixels : pixels + HALO, :] = cot_ref[0:HALO, :]
        msgn_ref[pixels : pixels + HALO, :] = cot_ref[pixels - HALO : pixels, :]
        at = pixels + HALO
        msgp_ref[at : at + STAT, :] = pack_stats(to_ref[0:1, :], to_ref[nb : nb + 1, :])
        msgn_ref[at : at + STAT, :] = pack_stats(to_ref[nb - 1 : nb, :], to_ref[2 * nb - 1 : 2 * nb, :])
    else:
        send_rows(out_ref, to_ref, nb, msgp_ref, msgn_ref)
    for save in saves:
        save.wait()


def conv_scratch(pixels, chans, nb, w_shape):
    rows = pixels + 2 * HALO + 16
    return [
        pltpu.VMEM((rows, chans), f32),
        pltpu.VMEM((rows, chans), f32),
        pltpu.VMEM((rows, chans), f32),
        pltpu.VMEM((pixels, 9 * chans), bf16),
        pltpu.VMEM(w_shape, bf16),
        pltpu.VMEM((2 * nb, chans), f32),
    ]


def conv_forward(x, recv_p, recv_n, t, amat, gain, bias, mask, ints, weight, cb, resid=None, cot=None):
    pixels, chans = x.shape
    nb = pixels // BLK
    last = resid is not None
    msg = sds((pixels + HALO + STAT, chans), bf16) if last else sds((HALO + 8, chans), f32)
    operands = [x, recv_p, recv_n, t, amat, gain, bias, mask, ints, weight.reshape(9 * chans, chans), cb]
    ins = [VM, VM, VM, VM, VM, VM, VM, VM, SM, HB, VM]
    if last:
        operands += [resid, cot]
        ins += [VM, VM]
    stats = sds((2 * nb, chans), f32)
    outs = [(sds((pixels, chans), f32), VM), (stats, VM), (stats, VM), (msg, VM), (msg, VM)]
    outs.append((sds((pixels, 9 * chans), bf16), HB))
    scratch = conv_scratch(pixels, chans, nb, (9 * chans, chans))
    scratch += [pltpu.SemaphoreType.DMA, pltpu.SemaphoreType.DMA((pixels // CHUNK,))]
    flops = 18 * pixels * chans * chans
    return call(functools.partial(conv_forward_kernel, nb, last), ins, outs, scratch, operands, flops)


def attention_kernel(nb, *refs):
    (
        x_ref, rp_ref, rn_ref, t_ref, amat_ref, gain_ref, bias_ref, ints_ref, img_ref,
        wq_ref, wk_ref, wv_ref, wp_ref, bq_ref, bv_ref, bp_ref, cot_ref,
    ) = refs[:17]
    (
        norm_hbm, dk_hbm, dv_hbm, out_ref, attn_ref, dq_ref, u_ref, stat_ref, to_ref, vec_ref, msgp_ref, msgn_ref,
    ) = refs[17:29]
    norm_ref, dk_ref, dv_ref, q_ref, k_ref, v_ref, da_ref, at_ref, dqf_ref, dkf_ref, dvf_ref, e_ref, h_ref, sems = refs[29:]
    pixels, chans = x_ref.shape
    own = pixels // CHUNK
    scale = 1.0 / math.sqrt(chans)
    amat = amat_ref[...]
    at = pixels + HALO
    prev_stats = unpack_stats(rp_ref[at : at + STAT, :])
    next_stats = unpack_stats(rn_ref[at : at + STAT, :])
    norm_stats(t_ref, nb, amat, prev_stats, next_stats, stat_ref)
    gain, bias = gain_ref[...], bias_ref[...]
    chunk_lo = ints_ref[1, 0] // CHUNK
    chunk_hi = (ints_ref[2, nb - 1] + CHUNK - 1) // CHUNK
    copies = []

    def send(scratch, hbm, which, c):
        r = pl.ds(c * CHUNK, CHUNK)
        copy = pltpu.make_async_copy(scratch.at[r, :], hbm.at[r, :], sems.at[which, c])
        copy.start()
        copies.append(copy)

    def xhat(c, b):
        r = (c % own) * CHUNK + b * BLK
        if c < own:
            x, k = rp_ref[r : r + BLK, :].astype(f32), 0
        elif c < 2 * own:
            x, k = x_ref[r : r + BLK, :], r // BLK
        else:
            x, k = rn_ref[r : r + BLK, :].astype(f32), nb - 1
        mean, inv = block_stats(stat_ref, nb, k)
        return (x - mean) * inv

    def reached(c, work, otherwise):
        if own <= c < 2 * own:
            work()
        else:
            inside = (c >= chunk_lo) & (c < chunk_hi)
            pl.when(inside)(work)
            pl.when(jnp.logical_not(inside))(otherwise)

    for c in range(3 * own):
        r = slice(c * CHUNK, (c + 1) * CHUNK)

        def keys(c=c, r=r):
            for b in range(CHUNK // BLK):
                norm_ref[c * CHUNK + b * BLK : c * CHUNK + (b + 1) * BLK, :] = (xhat(c, b) * gain + bias).astype(bf16)
            normed = norm_ref[r, :]
            k_ref[r, :] = dot_nn(normed, wk_ref[...]).astype(bf16)
            v_ref[r, :] = (dot_nn(normed, wv_ref[...]) + bv_ref[...]).astype(bf16)
            dkf_ref[r, :] = jnp.zeros((CHUNK, chans), f32)
            dvf_ref[r, :] = jnp.zeros((CHUNK, chans), f32)
            if own <= c < 2 * own:
                o = slice((c - own) * CHUNK, (c - own + 1) * CHUNK)
                q_ref[o, :] = (dot_nn(normed, wq_ref[...]) + bq_ref[...]).astype(bf16)
                da_ref[o, :] = dot_nt(cot_ref[o, :], wp_ref[...]).astype(bf16)

        def nothing(r=r):
            norm_ref[r, :] = jnp.zeros((CHUNK, chans), bf16)

        reached(c, keys, nothing)
        send(norm_ref, norm_hbm, 0, c)
    q_ref[pixels : pixels + CHUNK, :] = jnp.zeros((CHUNK, chans), bf16)
    da_ref[pixels : pixels + CHUNK, :] = jnp.zeros((CHUNK, chans), bf16)

    def attend(count, key_at, row_at, row_end):
        rows = pl.ds(pl.multiple_of(row_at, BLK), CHUNK)
        cols = pl.ds(pl.multiple_of(key_at, BLK), count)
        s = dot_nt(q_ref[rows, :], k_ref[cols, :]) * scale
        p = jnp.exp(s - jnp.max(s, axis=1, keepdims=True))
        at_row = lax.broadcasted_iota(jnp.int32, (CHUNK, 1), 0) + row_at
        p = p * jnp.where(at_row < row_end, 1.0 / jnp.sum(p, axis=1, keepdims=True), 0.0)
        low = p.astype(bf16)
        d_attn = da_ref[rows, :]
        dp = dot_nt(d_attn, v_ref[cols, :])
        at_ref[rows, :] = dot_nn(low, v_ref[cols, :]).astype(bf16)
        dvf_ref[cols, :] += dot_tn(low, d_attn)
        ds = (p * (dp - jnp.sum(p * dp, axis=1, keepdims=True))).astype(bf16)
        dqf_ref[rows, :] = (dot_nn(ds, k_ref[cols, :]) * scale).astype(bf16)
        dkf_ref[cols, :] += dot_tn(ds, q_ref[rows, :])

    def image(m, carry):
        key_at, side, begin, end = (img_ref[t, m] for t in range(4))
        for kind in (GRID // 2, 3 * GRID // 4, GRID):

            @pl.when(side == kind)
            def _():
                def block(i, inner):
                    attend(kind * kind, key_at, begin + i * CHUNK, end)
                    return inner

                lax.fori_loop(0, (end - begin + CHUNK - 1) // CHUNK, block, 0)

        return carry

    lax.fori_loop(0, img_ref[4, 0], image, 0)
    h_ref[...] = jnp.zeros(h_ref.shape, f32)
    for c in range(3 * own):
        r = slice(c * CHUNK, (c + 1) * CHUNK)
        o = slice((c % own) * CHUNK, (c % own + 1) * CHUNK)

        def fold(c=c, r=r, o=o):
            d_key = (dkf_ref[r, :] * scale).astype(bf16)
            d_value = dvf_ref[r, :].astype(bf16)
            dk_ref[r, :] = d_key
            dv_ref[r, :] = d_value
            u = dot_nt(d_key, wk_ref[...]) + dot_nt(d_value, wv_ref[...])
            if own <= c < 2 * own:
                d_query = dqf_ref[o, :]
                dq_ref[o, :] = d_query
                attn = at_ref[o, :]
                attn_ref[o, :] = attn
                out_ref[o, :] = (x_ref[o, :] + dot_nn(attn, wp_ref[...]) + bp_ref[...]).astype(bf16)
                u_ref[o, :] = u + dot_nt(d_query, wq_ref[...])
                for b in range(CHUNK // BLK):
                    k = (c - own) * (CHUNK // BLK) + b
                    u = u_ref[k * BLK : (k + 1) * BLK, :]
                    set_sums(e_ref, nb, k, u, u * xhat(c, b))
            else:
                msg_ref, row = (msgp_ref, 0) if c < own else (msgn_ref, 2)
                msg_ref[o, :] = u.astype(bf16)
                for b in range(CHUNK // BLK):
                    part = u[b * BLK : (b + 1) * BLK, :]
                    h_ref[row : row + 1, :] += jnp.sum(part, axis=0, keepdims=True)
                    h_ref[row + 1 : row + 2, :] += jnp.sum(part * xhat(c, b), axis=0, keepdims=True)

        def nothing(c=c, r=r, o=o):
            zero = jnp.zeros((CHUNK, chans), bf16)
            dk_ref[r, :] = zero
            dv_ref[r, :] = zero
            (msgp_ref if c < own else msgn_ref)[o, :] = zero

        reached(c, fold, nothing)
        send(dk_ref, dk_hbm, 1, c)
        send(dv_ref, dv_hbm, 2, c)
    before, before_x, after, after_x = (h_ref[i : i + 1, :] for i in range(4))
    d_bias = jnp.sum(e_ref[0:nb, :], axis=0, keepdims=True) + before + after
    d_gain = jnp.sum(e_ref[nb : 2 * nb, :], axis=0, keepdims=True) + before_x + after_x
    vec_ref[...] = stat_rows(d_gain, d_bias)
    e_ref[0:1, :] += before
    e_ref[nb : nb + 1, :] += before_x
    e_ref[nb - 1 : nb, :] += after
    e_ref[2 * nb - 1 : 2 * nb, :] += after_x
    e_ref[...] = e_ref[...] * gain
    own_totals(e_ref, nb, amat, to_ref)
    msgp_ref[pixels : pixels + HALO, :] = u_ref[0:HALO, :].astype(bf16)
    msgn_ref[pixels : pixels + HALO, :] = u_ref[pixels - HALO : pixels, :].astype(bf16)
    msgp_ref[at : at + STAT, :] = pack_stats(to_ref[0:1, :], to_ref[nb : nb + 1, :])
    msgn_ref[at : at + STAT, :] = pack_stats(to_ref[nb - 1 : nb, :], to_ref[2 * nb - 1 : 2 * nb, :])
    for copy in copies:
        copy.wait()


def attention(x, recv_p, recv_n, t, amat, gain, bias, ints, images, wq, wk, wv, wp, bq, bv, bp, cot):
    pixels, chans = x.shape
    nb, ext = pixels // BLK, 3 * pixels
    rows16, rows32 = sds((pixels, chans), bf16), sds((pixels, chans), f32)
    ext16 = sds((ext, chans), bf16)
    stats = sds((2 * nb, chans), f32)
    msg = sds((pixels + HALO + STAT, chans), bf16)
    outs = [(ext16, HB)] * 3
    outs += [(o, VM) for o in (rows16, rows16, rows16, rows32, stats, stats, sds((8, chans), f32), msg, msg)]
    padded = pltpu.VMEM((pixels + CHUNK, chans), bf16)
    window = pltpu.VMEM((ext, chans), bf16)
    wide = pltpu.VMEM((ext, chans), f32)
    scratch = [window, window, window, padded, window, window, padded, padded, padded, wide, wide]
    scratch += [pltpu.VMEM((2 * nb, chans), f32), pltpu.VMEM((8, chans), f32)]
    scratch.append(pltpu.SemaphoreType.DMA((3, ext // CHUNK)))
    ins = [VM] * 7 + [SM, SM] + [VM] * 8
    operands = (x, recv_p, recv_n, t, amat, gain, bias, ints, images, wq, wk, wv, wp, bq, bv, bp, cot)
    flops = 2 * pixels * chans * (chans * 9 + 6 * 1280)
    return call(functools.partial(attention_kernel, nb), ins, outs, scratch, operands, flops)


def conv_backward_kernel(nb, first, *refs):
    refs = refs[1:]
    if first:
        u_ref, mine_p_ref, mine_n_ref, rp_ref, rn_ref, xp_ref, xn_ref, cot_ref = refs[:8]
        refs = refs[8:]
    else:
        u_ref, rp_ref, rn_ref, xp_ref, xn_ref = refs[:5]
        refs = refs[5:]
    x_ref, stat_ref, s_ref, gain_ref, amat_ref, mask_ref, ints_ref, w_hbm = refs[:8]
    y_ref, ystat_ref, ygain_ref, ybias_ref = refs[8:12]
    refs = refs[12:]
    refs = refs[1:]
    if first:
        mid_out_ref, refs = refs[0], refs[1:]
    err_ref, v_ref, so_ref, vec_ref, msgp_ref, msgn_ref = refs[:6]
    mid_ref, left_ref, right_ref, patch_ref, w_ref, e_ref, w_sem = refs[6:]
    pixels, chans = x_ref.shape
    loads = []
    for tap in range(9):
        load = pltpu.make_async_copy(
            w_hbm.at[8 - tap], w_ref.at[:, pl.ds(tap * chans, chans)], w_sem.at[tap]
        )
        load.start()
        loads.append(load)
    amat = amat_ref[...]
    if first:
        at = pixels + HALO
        prev_stats = unpack_stats(rp_ref[at : at + STAT, :])
        next_stats = unpack_stats(rn_ref[at : at + STAT, :])
    else:
        prev_stats, next_stats = get_stats(rp_ref, HALO), get_stats(rn_ref, HALO)
    one, two = totals(s_ref, nb, amat, prev_stats, next_stats)
    e_ref[0:nb, :] = one
    e_ref[nb : 2 * nb, :] = two
    gain = gain_ref[...]

    def grad(u, x, k):
        mean, inv = block_stats(stat_ref, nb, k)
        m_one, m_two = block_stats(e_ref, nb, k)
        return inv * (u * gain - m_one - (x - mean) * inv * m_two)

    if first:
        low, high = slice(pixels - HALO, pixels), slice(0, HALO)
        side = slice(pixels, pixels + HALO)
        u = mine_p_ref[low, :].astype(f32) + rp_ref[side, :].astype(f32)
        before = xp_ref[side, :].astype(f32) + grad(u, xp_ref[low, :].astype(f32), 0)
        u = mine_n_ref[high, :].astype(f32) + rn_ref[side, :].astype(f32)
        after = xn_ref[side, :].astype(f32) + grad(u, xn_ref[high, :].astype(f32), nb - 1)
    else:
        before = grad(rp_ref[0:HALO, :], xp_ref[0:HALO, :], 0)
        after = grad(rn_ref[0:HALO, :], xn_ref[0:HALO, :], nb - 1)
    mid_ref[8 : 8 + HALO, :] = before.astype(bf16).astype(f32)
    mid_ref[8 + HALO + pixels : 8 + 2 * HALO + pixels, :] = after.astype(bf16).astype(f32)
    column = jnp.zeros((1, chans), f32)
    for k in range(nb):
        r = slice(k * BLK, (k + 1) * BLK)
        u = u_ref[r, :]
        if first:
            u = u + rp_ref[r, :].astype(f32) + rn_ref[r, :].astype(f32)
        g = grad(u, x_ref[r, :], k)
        if first:
            g = g + cot_ref[r, :].astype(f32)
            mid_out_ref[r, :] = g
        low = g.astype(bf16)
        err_ref[r, :] = low
        g = low.astype(f32)
        column = column + jnp.sum(g, axis=0, keepdims=True)
        mid_ref[8 + HALO + k * BLK : 8 + HALO + (k + 1) * BLK, :] = g
    shift_columns(mid_ref, left_ref, right_ref, pixels + 2 * HALO)
    y_gain, y_bias = ygain_ref[...], ybias_ref[...]
    for c in range(0, pixels, CHUNK):
        for k in range(c // BLK, (c + CHUNK) // BLK):
            make_patch((left_ref, mid_ref, right_ref), patch_ref, mask_ref, ints_ref, k, chans)
        if c == 0:
            for load in loads:
                load.wait()
        v_ref[c : c + CHUNK, :] = dot_nt(patch_ref[c : c + CHUNK, :], w_ref[...])
        for k in range(c // BLK, (c + CHUNK) // BLK):
            r = slice(k * BLK, (k + 1) * BLK)
            mean, inv = block_stats(ystat_ref, nb, k)
            xh = (y_ref[r, :] - mean) * inv
            v = v_ref[r, :] * silu_slope(xh * y_gain + y_bias)
            v_ref[r, :] = v
            set_sums(e_ref, nb, k, v, v * xh)
    d_bias = jnp.sum(e_ref[0:nb, :], axis=0, keepdims=True)
    d_gain = jnp.sum(e_ref[nb : 2 * nb, :], axis=0, keepdims=True)
    vec_ref[...] = jnp.concatenate([d_gain, d_bias, column, jnp.zeros((5, chans), f32)], axis=0)
    e_ref[...] = e_ref[...] * y_gain
    own_totals(e_ref, nb, amat, so_ref)
    if first:
        send_rows(v_ref, so_ref, nb, msgp_ref, msgn_ref)
    else:
        send_stats(so_ref, nb, msgp_ref, msgn_ref, 0)


def conv_backward(first, token, heads, x, stat, s, gain, amat, mask, ints, weight, y, ystat, ygain, ybias):
    pixels, chans = x.shape
    nb = pixels // BLK
    operands = [token, *heads, x, stat, s, gain, amat, mask, ints, weight.reshape(9, chans, chans), y, ystat, ygain, ybias]
    ins = [HB] + [VM] * len(heads) + [VM] * 6 + [SM, HB] + [VM] * 4
    msg = sds((HALO + 8 if first else 8, chans), f32)
    rows = sds((pixels, chans), f32)
    outs = [sds(token.shape, token.dtype)] + ([rows] if first else [])
    outs += [sds((pixels, chans), bf16), rows, sds((2 * nb, chans), f32), sds((8, chans), f32), msg, msg]
    scratch = conv_scratch(pixels, chans, nb, (chans, 9 * chans)) + [pltpu.SemaphoreType.DMA((9,))]
    flops = 18 * pixels * chans * chans
    return call(
        functools.partial(conv_backward_kernel, nb, first), ins, [(outs[0], HB)] + [(o, VM) for o in outs[1:]], scratch,
        operands, flops, aliases={0: 0},
    )


def tail_kernel(nb, passes, *refs):
    v_ref, rp_ref, rn_ref, s_ref, x_ref, stat_ref, gain_ref, amat_ref, mid_ref, w_ref = refs[passes : passes + 10]
    err_ref, fg_ref, vec_ref, e_ref = refs[2 * passes + 10 :]
    pixels, chans = x_ref.shape
    one, two = totals(s_ref, nb, amat_ref[...], get_stats(rp_ref, 0), get_stats(rn_ref, 0))
    e_ref[0:nb, :] = one
    e_ref[nb : 2 * nb, :] = two
    gain = gain_ref[...]
    column = jnp.zeros((1, chans), f32)
    for c in range(0, pixels, CHUNK):
        for k in range(c // BLK, (c + CHUNK) // BLK):
            r = slice(k * BLK, (k + 1) * BLK)
            mean, inv = block_stats(stat_ref, nb, k)
            m_one, m_two = block_stats(e_ref, nb, k)
            g = mid_ref[r, :] + inv * (v_ref[r, :] * gain - m_one - (x_ref[r, :] - mean) * inv * m_two)
            low = g.astype(bf16)
            err_ref[r, :] = low
            column = column + jnp.sum(low.astype(f32), axis=0, keepdims=True)
        fg_ref[c : c + CHUNK, :] = dot_nt(err_ref[c : c + CHUNK, :], w_ref[...]).astype(bf16)
    vec_ref[...] = jnp.concatenate([column, jnp.zeros((7, chans), f32)], axis=0)


def tail(passed, v, recv_p, recv_n, s, x, stat, gain, amat, mid, w_in):
    pixels, chans = x.shape
    nb = pixels // BLK
    count = len(passed)
    outs = [(sds(a.shape, a.dtype), HB) for a in passed]
    outs += [(sds((pixels, chans), bf16), VM), (sds((pixels, w_in.shape[0]), bf16), VM), (sds((8, chans), f32), VM)]
    operands = (*passed, v, recv_p, recv_n, s, x, stat, gain, amat, mid, w_in)
    scratch = [pltpu.VMEM((2 * nb, chans), f32)]
    flops = 2 * pixels * chans * w_in.shape[0]
    body = functools.partial(tail_kernel, nb, count)
    aliases = {i: i for i in range(count)}
    return call(body, [HB] * count + [VM] * 10, outs, scratch, operands, flops, aliases=aliases)


def finish_kernel(places, tokens, *refs):
    up_ref, mine_hbm, other_hbm, *out_refs, read_ref, stage_ref, read_sems, sems = refs[tokens:]
    slots = stage_ref.shape[0]

    def write(own):
        work = []
        for source, half in ((mine_hbm, own), (other_hbm, 1 - own)):
            for row, moves in places(half, out_refs):
                work.append((source.at[pl.ds(row, CHUNK), :], moves))
        reads = [
            pltpu.make_async_copy(source, read_ref.at[i % slots], read_sems.at[i % slots])
            for i, (source, _) in enumerate(work)
        ]
        for read in reads[:slots]:
            read.start()
        pending = [[] for _ in range(slots)]
        for i, (_, moves) in enumerate(work):
            slot = i % slots
            reads[i].wait()
            for copy in pending[slot]:
                copy.wait()
            stage_ref[slot] = read_ref[slot].astype(f32)
            if i + slots < len(work):
                reads[i + slots].start()
            pending[slot] = []
            for k, (lanes, target) in enumerate(moves):
                copy = pltpu.make_async_copy(stage_ref.at[slot, :, lanes], target, sems.at[slot, k])
                copy.start()
                pending[slot].append(copy)
        for copies in pending:
            for copy in copies:
                copy.wait()

    for own in range(2):
        pl.when(up_ref[0] == own)(functools.partial(write, own))


def finish(places, up, mine, outs, tokens=()):
    chans = mine.shape[1]
    slots = 16
    scratch = [pltpu.VMEM((slots, CHUNK, chans), bf16), pltpu.VMEM((slots, CHUNK, chans), f32)]
    scratch += [pltpu.SemaphoreType.DMA((slots,)), pltpu.SemaphoreType.DMA((slots, 2))]
    body = functools.partial(finish_kernel, places, len(tokens))
    operands = (*tokens, up.reshape(1), mine, partner(mine, "rows", 1))
    return call(body, [HB] * len(tokens) + [SM, HB, HB], [(o, HB) for o in outs], scratch, operands, 0)


def conv_places(half, out_ref):
    rows = out_ref.shape[0] // 2
    return [(r, [(slice(None), out_ref.at[pl.ds(half * rows + r, CHUNK), :])]) for r in range(0, rows, CHUNK)]


def early_places(half, out_refs):
    conv_ref, *squares = out_refs
    out = conv_places(half, conv_ref)
    row = conv_ref.shape[0] // 2
    for ref in squares[2 * half : 2 * half + 2]:
        for r in range(0, ref.shape[0], CHUNK):
            out.append((row, [(slice(None), ref.at[pl.ds(r, CHUNK), :])]))
            row += CHUNK
    return out


def late_places(half, out_refs):
    conv_ref, in_ref, vec_ref = out_refs
    return conv_places(half, conv_ref) + [(conv_ref.shape[0] // 2, [(slice(None), (in_ref, vec_ref)[half])])]


def book_places(half, out_refs):
    (book_ref,) = out_refs
    quarter, emb = book_ref.shape[0] // 4, book_ref.shape[1]
    out = []
    for r in range(0, quarter, CHUNK):
        to = half * quarter + r
        left = (pl.ds(0, emb), book_ref.at[pl.ds(to, CHUNK), :])
        right = (pl.ds(emb, emb), book_ref.at[pl.ds(2 * quarter + to, CHUNK), :])
        out.append((r, [left, right]))
    return out


def along(array, axis, by):
    count = lax.axis_size(axis)
    return lax.ppermute(array, axis, [(i, i + by) for i in range(count) if 0 <= i + by < count])


def around(array, axis, by):
    count = lax.axis_size(axis)
    return lax.ppermute(array, axis, [(i, (i + by) % count) for i in range(count)])


def swap(to_prev, to_next):
    return along(to_next, "rows", 1), along(to_prev, "rows", -1)


def partner(array, axis, bit):
    return lax.ppermute(array, axis, [(i, i ^ bit) for i in range(lax.axis_size(axis))])


def bits(axis):
    return [(axis, 1 << b) for b in range(lax.axis_size(axis).bit_length() - 1)]


def half_of(x, which):
    return lax.dynamic_slice_in_dim(x, which * (x.shape[0] // 2), x.shape[0] // 2)


def core_send(arrays):
    up = lax.axis_index("rows") % 2
    send = [half_of(x, 1 - up) for x in arrays]
    return partner(jnp.concatenate(send) if len(send) > 1 else send[0], "rows", 1)


def add(one, two):
    return (one.astype(f32) + two.astype(f32)).astype(bf16)


def join(parts):
    return jnp.concatenate(parts) if len(parts) > 1 else parts[0]


def exchange(axis, bit, jobs):
    up = (lax.axis_index(axis) // bit) % 2
    keep = [half_of(x, up) if reduce else x for reduce, x in jobs]
    got = partner(join([half_of(x, 1 - up) if reduce else x for reduce, x in jobs]), axis, bit)
    at, out = 0, []
    for (reduce, _), x in zip(jobs, keep):
        other = got[at : at + x.shape[0]]
        at += x.shape[0]
        if reduce:
            out.append(add(x, other))
        else:
            out.append(jnp.where(up == 0, jnp.concatenate([x, other]), jnp.concatenate([other, x])))
    return out


def plan(flip, *axes):
    middle = bits(axes[0])[1:]
    steps = (middle[::-1] if flip else middle) + [step for axis in axes[1:] for step in bits(axis)]
    return [(step, True) for step in steps] + [(step, False) for step in steps[::-1]]


def rounds(arrays, plans, begins, turns=None):
    arrays = list(arrays)
    for turn in turns or range(max(begin + len(p) for p, begin in zip(plans, begins))):
        by_partner = {}
        for i, (p, begin) in enumerate(zip(plans, begins)):
            if 0 <= turn - begin < len(p):
                step, reduce = p[turn - begin]
                by_partner.setdefault((begin, *step), []).append((i, reduce))
        for (_, *step), jobs in by_partner.items():
            out = exchange(*step, [(reduce, arrays[i]) for i, reduce in jobs])
            for (i, _), x in zip(jobs, out):
                arrays[i] = x
    return arrays


def streams(x, *axes):
    world = math.prod(lax.axis_size(axis) for axis in axes) // 2
    unit = 16 * world
    cut = -(-x.shape[0] // (2 * unit)) * unit
    return [x[:cut], x[cut:]]


def half_of(x, which):
    return lax.dynamic_slice_in_dim(x, which * (x.shape[0] // 2), x.shape[0] // 2)


def core_swap(x):
    up = lax.axis_index("rows") % 2
    return half_of(x, up), partner(half_of(x, 1 - up), "rows", 1)


def per_device(
    features, indices, img_width, img_start, codebook, w_in, b_in, gn1_gain, gn1_bias, conv1_w, conv1_b,
    gn2_gain, gn2_bias, conv2_w, conv2_b, gn3_gain, gn3_bias, w_query, b_query, w_key, w_value, b_value,
    w_proj, b_proj, cotangent,
):
    pixels, emb = features.shape[1], features.shape[2]
    chans = w_in.shape[1]
    nb = pixels // BLK
    widths, starts = img_width[0], img_start[0]
    first_pos = lax.axis_index("rows") * pixels
    row = lambda v: v.reshape(1, -1)

    positions = first_pos + jnp.arange(pixels, dtype=jnp.int32)
    image_id = jnp.sum((starts[None, :] <= positions[:, None]).astype(jnp.int32), axis=1) - 1
    choose = image_id[:, None] == jnp.arange(widths.shape[0], dtype=jnp.int32)[None, :]
    side = jnp.sum(jnp.where(choose, widths[None, :], 0), axis=1)
    begin = jnp.sum(jnp.where(choose, starts[None, :], 0), axis=1)
    offset = positions - begin
    safe = jnp.maximum(side, 1)
    row_at, col_at = offset // safe, offset % safe
    valid = []
    for dr in (-1, 0, 1):
        for dc in (-1, 0, 1):
            r, c = row_at + dr, col_at + dc
            valid.append((r >= 0) & (r < side) & (c >= 0) & (c < side))
    mask = jnp.stack(valid, axis=1).astype(f32)
    low_key = begin - first_pos + pixels
    spans = jnp.stack([low_key, low_key + side * side], axis=1)
    block_id = image_id[::BLK]
    ints = jnp.stack([side[::BLK], spans[::BLK, 0], spans[::BLK, 1]])
    count = (jnp.maximum(side * side, 1)[::BLK] * (chans // GN_GROUPS)).astype(f32)
    amat = jnp.concatenate(
        [
            (block_id[:, None] == block_id[None, :]).astype(f32),
            (block_id == block_id[0]).astype(f32)[:, None],
            (block_id == block_id[-1]).astype(f32)[:, None],
            (1.0 / count)[:, None],
        ],
        axis=1,
    )

    at_image = jnp.minimum(block_id[0] + jnp.arange(8, dtype=jnp.int32), widths.shape[0] - 1)
    pick = at_image[:, None] == jnp.arange(widths.shape[0], dtype=jnp.int32)[None, :]
    img_side = jnp.sum(jnp.where(pick, widths[None, :], 0), axis=1)
    img_at = jnp.sum(jnp.where(pick, starts[None, :], 0), axis=1) - first_pos
    images = jnp.stack(
        [
            img_at + pixels,
            img_side,
            jnp.maximum(img_at, 0),
            jnp.minimum(img_at + img_side * img_side, pixels),
            jnp.broadcast_to(block_id[-1] - block_id[0] + 1, (8,)),
        ]
    )

    groups = lax.axis_size("chan")
    codes = codebook.shape[0]
    ring = [indices[0]] + [around(indices, "chan", -d)[0] for d in range(1, groups)]
    local = [index - lax.axis_index("chan") * codes for index in ring]
    found = [lookup(index[:, None], codebook) for index in local[1:]]
    found.insert(0, lookup(local[0][:, None], codebook, found))
    rows_in = [found[0]] + [around(found[d], "chan", d) for d in range(1, groups)]

    stats2 = sds((2 * nb, chans), f32)
    rows32 = sds((pixels, chans), f32)
    msg32 = sds((HALO + 8, chans), f32)
    quant, resid_in, t_one, to_p, to_n = call(
        functools.partial(lift_kernel, groups, nb),
        [VM] * (4 + groups),
        [(o, VM) for o in (sds((pixels, emb), bf16), rows32, stats2, msg32, msg32)],
        [pltpu.VMEM((2 * nb, chans), f32)],
        (features[0], *rows_in, w_in, row(b_in), amat),
        2 * pixels * emb * chans,
    )
    p_one, n_one = swap(to_p, to_n)
    hid_one, stat_one, t_two, to_p, to_n, patch_one = conv_forward(
        resid_in, p_one, n_one, t_one, amat, row(gn1_gain), row(gn1_bias), mask, ints, conv1_w, row(conv1_b)
    )
    p_two, n_two = swap(to_p, to_n)
    cot = cotangent[0]
    resid_mid, stat_two, t_three, to_p, to_n, patch_two = conv_forward(
        hid_one, p_two, n_two, t_two, amat, row(gn2_gain), row(gn2_bias), mask, ints, conv2_w, row(conv2_b),
        resid_in, cot,
    )
    p_three, n_three = swap(to_p, to_n)
    normed, d_key, d_value, output, attn, d_query, u_own, stat_three, s_three, vec_three, to_p, to_n = attention(
        resid_mid, p_three, n_three, t_three, amat, row(gn3_gain), row(gn3_bias), ints, images,
        w_query, w_key, w_value, w_proj, row(b_query), row(b_value), row(b_proj), cot,
    )
    p_back, n_back = swap(to_p, to_n)
    tn = lambda a, b: jnp.einsum("nk,nc->kc", a, b, preferred_element_type=f32).astype(bf16)
    own_normed = normed[pixels : 2 * pixels]
    g_proj = tn(attn, cot)
    g_query = tn(own_normed, d_query)
    g_key = tn(normed, d_key)
    g_value = tn(normed, d_value)
    g_attn = jnp.concatenate([g_proj, g_query, g_key, g_value])
    g_b_proj = jnp.sum(cot.astype(f32), axis=0, keepdims=True)
    g_b_query = jnp.sum(d_query.astype(f32), axis=0, keepdims=True)
    g_b_value = jnp.sum(d_value.astype(f32), axis=0, keepdims=True)
    g_attn, d_mid, err_two, v_two, s_two, vec_two, msg_p, msg_n = conv_backward(
        True, g_attn, (u_own, to_p, to_n, p_back, n_back, p_three, n_three, cot),
        resid_mid, stat_three, s_three, row(gn3_gain), amat, mask, ints, conv2_w,
        hid_one, stat_two, row(gn2_gain), row(gn2_bias),
    )
    p_four, n_four = swap(msg_p, msg_n)
    g_conv2 = tn(patch_two, err_two)
    g_conv2, err_one, v_one, s_one, vec_one, msg_p, msg_n = conv_backward(
        False, g_conv2, (v_two, p_four, n_four, p_two, n_two),
        hid_one, stat_two, s_two, row(gn2_gain), amat, mask, ints, conv1_w,
        resid_in, stat_one, row(gn1_gain), row(gn1_bias),
    )
    p_five, n_five = swap(msg_p, msg_n)
    err_one, g_conv2, g_attn, err_in, feature_grad, vec_in = tail(
        (err_one, g_conv2, g_attn), v_one, p_five, n_five, s_one, resid_in, stat_one, row(gn1_gain), amat, d_mid, w_in
    )
    below, above = [feature_grad], [feature_grad]
    for _ in range(1, groups):
        below.append(along(below[-1], "chan", 1))
        above.append(along(above[-1], "chan", -1))
    two = jnp.concatenate([add(*core_swap(g_conv2)), add(*core_swap(g_attn))])
    g_conv1 = tn(patch_one, err_one)
    vectors = (vec_in, vec_one, vec_two, vec_three, g_b_query, g_b_value, g_b_proj)
    g_conv1, begun, small = own_part(g_conv1, two, row(local[0]), feature_grad, quant, err_in, vectors, codes)
    one = add(*core_swap(g_conv1))
    small = add(*core_swap(small))
    both = [plan(flip, "rows", "chan") for flip in (False, True)]
    plans = both + both + both[1:] + [plan(flip, "rows") for flip in (False, True)]
    begins = [0, 0, LATE_ROUND, LATE_ROUND, LATE_ROUND, BOOK_ROUND, BOOK_ROUND]
    pair = lambda d: (row(local[groups - d]), (below[d], above[groups - d]))
    middle = [pair(d) for d in range(1, groups) if 2 * d == groups]
    outer = [pair(d) for d in range(1, groups) if 2 * d != groups]
    work = rounds(streams(two, "rows", "chan"), plans[:2], begins, range(1))
    book = scatter(*zip(*middle), codes, f32, begun, work)
    work = rounds(work, plans[:2], begins, range(1, 2))
    book = scatter(*zip(*outer), codes, bf16, book, work)
    book = add(*core_swap(book))
    work += streams(one, "rows", "chan") + [small] + streams(book, "rows")
    turns = max(begin + len(p) for p, begin in zip(plans, begins))
    work = rounds(work, plans, begins, range(2, turns))
    up = lax.axis_index("rows") % 2
    square, conv = sds((chans, chans), f32), sds((9 * chans, chans), f32)
    early = finish(early_places, up, jnp.concatenate(work[:2]), [conv] + [square] * 4)
    book = finish(book_places, up, jnp.concatenate(work[5:]), [sds((codes, emb), f32)])
    narrow = [sds((emb, chans), f32), sds((chans - emb, chans), f32)]
    sum_one, s_in, vec = finish(
        late_places, up, jnp.concatenate(work[2:5]), [conv] + narrow, (early[0], book[0])
    )
    sum_two, s_proj, s_query, s_key, s_value = early
    (book_grad,) = book
    return (
        output[None],
        feature_grad[None],
        book_grad,
        s_in,
        vec[0],
        vec[1],
        vec[2],
        sum_one.reshape(conv1_w.shape),
        vec[3],
        vec[4],
        vec[5],
        sum_two.reshape(conv2_w.shape),
        vec[6],
        vec[7],
        vec[8],
        s_query,
        vec[9],
        s_key,
        s_value,
        vec[10],
        s_proj,
        vec[11],
    )


def solution(mesh):
    group, copied = P("chan", "rows", None), P()
    placed = (group, P("chan", "rows"), P("chan", None), P("chan", None), P("chan", None))
    return jax.shard_map(
        per_device,
        mesh=mesh,
        in_specs=placed + (copied,) * 19 + (group,),
        out_specs=(group, group, P("chan", None)) + (copied,) * 19,
        check_vma=False,
    )
```

```python
import functools
import math

import jax
import jax.numpy as jnp
from jax import lax
from jax.experimental import pallas as pl
from jax.experimental.pallas import tpu as pltpu
from jax.sharding import PartitionSpec as P

GN_GROUPS = 32
GRID = 32
BLK = (GRID // 4) ** 2
HALO = 64
CHUNK = 256
STAT = 16
epsilon = 1e-06
masked_score = -1e30
f32 = jnp.float32
bf16 = jnp.bfloat16
MIB = 1 << 20
LATE_ROUND = 2
BOOK_ROUND = 4

VM = pl.BlockSpec(memory_space=pltpu.VMEM)
SM = pl.BlockSpec(memory_space=pltpu.SMEM)
HB = pl.BlockSpec(memory_space=pl.ANY)


def call(body, ins, outs, scratch, operands, flops, vmem=58, aliases={}, light=False):
    bytes_all = sum(math.prod(a.shape) * a.dtype.itemsize for a in (*operands, *[o[0] for o in outs]))
    if light:
        flops = bytes_all = 0
    return pl.pallas_call(
        body,
        out_shape=[o[0] for o in outs],
        in_specs=ins,
        out_specs=[o[1] for o in outs],
        scratch_shapes=scratch,
        input_output_aliases=aliases,
        compiler_params=pltpu.CompilerParams(vmem_limit_bytes=vmem * MIB),
        cost_estimate=pl.CostEstimate(flops=flops, bytes_accessed=bytes_all, transcendentals=0),
    )(*operands)


def sds(shape, dtype):
    return jax.ShapeDtypeStruct(shape, dtype)


def dot_nn(a, b):
    return lax.dot_general(a, b, (((1,), (0,)), ((), ())), preferred_element_type=f32)


def dot_nt(a, b):
    return lax.dot_general(a, b, (((1,), (1,)), ((), ())), preferred_element_type=f32)


def dot_tn(a, b):
    return lax.dot_general(a, b, (((0,), (0,)), ((), ())), preferred_element_type=f32)


def group_total(x):
    per = x.shape[1] // GN_GROUPS
    lane = lax.broadcasted_iota(jnp.int32, x.shape, 1)
    step = 1
    while step < per:
        up = pltpu.roll(x, step, 1)
        down = pltpu.roll(x, x.shape[1] - step, 1)
        x = x + jnp.where((lane & step) != 0, up, down)
        step *= 2
    return x


def image_total(e_ref, row, nb, amat):
    total = amat[:, 0:1] * e_ref[row : row + 1, :]
    for j in range(1, nb):
        total = total + amat[:, j : j + 1] * e_ref[row + j : row + j + 1, :]
    return total


def split3(v):
    high = v.astype(bf16)
    rest = v - high.astype(f32)
    mid = rest.astype(bf16)
    low = (rest - mid.astype(f32)).astype(bf16)
    return high, mid, low


def pack_stats(a, b):
    rows = [p.astype(f32) for p in (*split3(a), *split3(b))]
    rows.append(jnp.zeros((STAT - 6, a.shape[1]), f32))
    return jnp.concatenate(rows, axis=0).astype(bf16)


def unpack_stats(block):
    v = block.astype(f32)
    return v[0:1] + v[1:2] + v[2:3], v[3:4] + v[4:5] + v[5:6]


def stat_rows(a, b):
    return jnp.concatenate([a, b, jnp.zeros((6, a.shape[1]), f32)], axis=0)


def totals(t_ref, nb, amat, prev_rows, next_rows):
    first, last = amat[:, nb : nb + 1], amat[:, nb + 1 : nb + 2]
    one = t_ref[0:nb, :] + first * prev_rows[0] + last * next_rows[0]
    two = t_ref[nb : 2 * nb, :] + first * prev_rows[1] + last * next_rows[1]
    inv_count = amat[:, nb + 2 : nb + 3]
    return one * inv_count, two * inv_count


def norm_stats(t_ref, nb, amat, prev_rows, next_rows, stat_ref):
    mean, square = totals(t_ref, nb, amat, prev_rows, next_rows)
    stat_ref[0:nb, :] = mean
    stat_ref[nb : 2 * nb, :] = lax.rsqrt(square - mean * mean + epsilon)


def block_stats(stat_ref, nb, k):
    return stat_ref[k : k + 1, :], stat_ref[nb + k : nb + k + 1, :]


def own_totals(e_ref, nb, amat, t_ref):
    t_ref[0:nb, :] = group_total(image_total(e_ref, 0, nb, amat))
    t_ref[nb : 2 * nb, :] = group_total(image_total(e_ref, nb, nb, amat))


def set_sums(e_ref, nb, k, x, y):
    e_ref[k : k + 1, :] = jnp.sum(x, axis=0, keepdims=True)
    e_ref[nb + k : nb + k + 1, :] = jnp.sum(y, axis=0, keepdims=True)


def silu(pre):
    return pre * jax.nn.sigmoid(pre)


def silu_slope(pre):
    s = jax.nn.sigmoid(pre)
    return s * (1.0 + pre * (1.0 - s))


def shift_columns(mid_ref, left_ref, right_ref, rows):
    left_ref[8 : 8 + rows, :] = mid_ref[7 : 7 + rows, :]
    right_ref[8 : 8 + rows, :] = mid_ref[9 : 9 + rows, :]


def make_patch(refs, patch_ref, mask_ref, ints_ref, k, chans):
    side = ints_ref[0, k]
    for dr in (-1, 0, 1):
        at = 8 + HALO + k * BLK
        if dr != 0:
            at = pl.multiple_of(at + dr * side, 8)
        for dc in (-1, 0, 1):
            tap = (dr + 1) * 3 + dc + 1
            rows = refs[dc + 1][pl.ds(at, BLK), :]
            if tap != 4:
                rows = rows * mask_ref[k * BLK : (k + 1) * BLK, tap : tap + 1]
            patch_ref[k * BLK : (k + 1) * BLK, tap * chans : (tap + 1) * chans] = rows.astype(bf16)


def lookup_kernel(tokens, *refs):
    index_ref, book_ref, out_ref = refs[tokens:]
    codes = book_ref.shape[0]
    total = jnp.zeros(out_ref.shape, f32)
    for c in range(0, codes, 512):
        lane = lax.broadcasted_iota(jnp.int32, (index_ref.shape[0], 512), 1) + c
        hot = jnp.where(index_ref[...] == lane, 1.0, 0.0).astype(bf16)
        total = total + dot_nn(hot, book_ref[c : c + 512, :])
    out_ref[...] = total.astype(bf16)


def lookup(index, book, tokens=()):
    pixels, emb = index.shape[0], book.shape[1]
    step = 256
    return pl.pallas_call(
        functools.partial(lookup_kernel, len(tokens)),
        grid=(pixels // step,),
        out_shape=sds((pixels, emb), bf16),
        in_specs=[HB] * len(tokens) + [pl.BlockSpec((step, 1), lambda i: (i, 0)), pl.BlockSpec(book.shape, lambda i: (0, 0))],
        out_specs=pl.BlockSpec((step, emb), lambda i: (i, 0)),
        compiler_params=pltpu.CompilerParams(vmem_limit_bytes=40 * MIB),
        cost_estimate=pl.CostEstimate(
            flops=2 * pixels * book.shape[0] * emb, bytes_accessed=book.size * 2, transcendentals=0
        ),
    )(*tokens, index, book)


def scatter_kernel(step, tokens, parts, *refs):
    index_refs, grad_refs = refs[tokens : tokens + parts], refs[tokens + parts : tokens + 3 * parts]
    begun_ref, out_ref = refs[-2:]
    half, emb = step * pl.num_programs(0), grad_refs[0].shape[1]
    for side in range(2):
        lanes = slice(side * emb, (side + 1) * emb)
        code = lax.broadcasted_iota(jnp.int32, (step, 512), 0) + (pl.program_id(0) * step + side * half)
        total = begun_ref[:, lanes]
        for index_ref, one_ref, two_ref in zip(index_refs, grad_refs[::2], grad_refs[1::2]):
            for p in range(0, one_ref.shape[0], 512):
                hot = jnp.where(index_ref[0:1, p : p + 512] == code, 1.0, 0.0).astype(bf16)
                grad = one_ref[p : p + 512, :].astype(f32) + two_ref[p : p + 512, :].astype(f32)
                total = total + dot_nn(hot, grad.astype(bf16))
        out_ref[:, lanes] = total.astype(out_ref.dtype)


def scatter(indices, pairs, codes, dtype, begun, tokens):
    grads = [x for pair in pairs for x in pair]
    emb, step, parts = grads[0].shape[1], 256, len(pairs)
    whole = [pl.BlockSpec(a.shape, lambda i: (0, 0)) for a in (*indices, *grads)]
    tile = pl.BlockSpec((step, 2 * emb), lambda i: (i, 0))
    return pl.pallas_call(
        functools.partial(scatter_kernel, step, len(tokens), parts),
        grid=(codes // 2 // step,),
        out_shape=sds((codes // 2, 2 * emb), dtype),
        in_specs=[HB for _ in tokens] + whole + [tile],
        out_specs=tile,
        compiler_params=pltpu.CompilerParams(vmem_limit_bytes=40 * MIB),
        cost_estimate=pl.CostEstimate(
            flops=2 * parts * grads[0].shape[0] * codes * emb, bytes_accessed=codes * emb * 8, transcendentals=0
        ),
    )(*tokens, *indices, *grads, begun)


def own_kernel(step, pass_ref, token_ref, index_ref, grad_ref, quant_ref, err_ref, in_ref, one_ref, two_ref, three_ref,
               query_ref, value_ref, proj_ref, passed_ref, out_ref, small_ref):
    emb = grad_ref.shape[1]
    half = out_ref.shape[0]
    for r in range(0, half, step):
        for side in range(2):
            code = lax.broadcasted_iota(jnp.int32, (step, 512), 0) + (r + side * half)
            total = jnp.zeros((step, emb), f32)
            for p in range(0, grad_ref.shape[0], 512):
                hot = jnp.where(index_ref[0:1, p : p + 512] == code, 1.0, 0.0).astype(bf16)
                total = total + dot_nn(hot, grad_ref[p : p + 512, :])
            out_ref[r : r + step, side * emb : (side + 1) * emb] = total
    small_ref[0:emb, :] = dot_tn(quant_ref[...], err_ref[...]).astype(bf16)
    rows = [in_ref[0:1, :], one_ref[0:3, :], two_ref[0:3, :], three_ref[0:2, :], query_ref[...], value_ref[...], proj_ref[...]]
    filler = jnp.zeros((small_ref.shape[0] - emb - 12, small_ref.shape[1]), f32)
    small_ref[emb:, :] = jnp.concatenate([*rows, filler], axis=0).astype(bf16)


def own_part(passed, token, index, grad, quant, err, vectors, codes):
    emb, chans = grad.shape[1], err.shape[1]
    outs = [(sds(passed.shape, bf16), HB), (sds((codes // 2, 2 * emb), f32), VM), (sds((chans, chans), bf16), VM)]
    operands = (passed, token, index, grad, quant, err, *vectors)
    flops = 2 * grad.shape[0] * emb * (codes + chans)
    return call(functools.partial(own_kernel, 256), [HB] * 2 + [VM] * (len(operands) - 2), outs, [], operands, flops, aliases={0: 0})


def lift_kernel(n_codes, nb, *refs):
    feat_ref, code_refs = refs[0], refs[1 : 1 + n_codes]
    w_ref, b_ref, amat_ref, quant_ref, resid_ref, t_ref, msgp_ref, msgn_ref, e_ref = refs[1 + n_codes :]
    pixels = feat_ref.shape[0]
    for c in range(0, pixels, CHUNK):
        at = slice(c, c + CHUNK)
        code = code_refs[0][at, :].astype(f32)
        for other in code_refs[1:]:
            code = code + other[at, :].astype(f32)
        quant = (feat_ref[at, :].astype(f32) + code).astype(bf16)
        quant_ref[at, :] = quant
        resid_ref[at, :] = dot_nn(quant, w_ref[...]) + b_ref[...]
    for k in range(nb):
        x = resid_ref[k * BLK : (k + 1) * BLK, :]
        set_sums(e_ref, nb, k, x, x * x)
    own_totals(e_ref, nb, amat_ref[...], t_ref)
    send_rows(resid_ref, t_ref, nb, msgp_ref, msgn_ref)


def send_rows(x_ref, t_ref, nb, msgp_ref, msgn_ref):
    pixels = x_ref.shape[0]
    msgp_ref[0:HALO, :] = x_ref[0:HALO, :]
    msgn_ref[0:HALO, :] = x_ref[pixels - HALO : pixels, :]
    send_stats(t_ref, nb, msgp_ref, msgn_ref, HALO)


def send_stats(t_ref, nb, msgp_ref, msgn_ref, at):
    msgp_ref[at : at + 8, :] = stat_rows(t_ref[0:1, :], t_ref[nb : nb + 1, :])
    msgn_ref[at : at + 8, :] = stat_rows(t_ref[nb - 1 : nb, :], t_ref[2 * nb - 1 : 2 * nb, :])


def get_stats(ref, at):
    return ref[at : at + 1, :], ref[at + 1 : at + 2, :]


def conv_forward_kernel(nb, last, *refs):
    x_ref, rp_ref, rn_ref, t_ref, amat_ref, gain_ref, bias_ref, mask_ref, ints_ref, w_hbm, cb_ref = refs[:11]
    refs = refs[11:]
    if last:
        resid_ref, cot_ref = refs[:2]
        refs = refs[2:]
    out_ref, stat_ref, to_ref, msgp_ref, msgn_ref, patch_hbm = refs[:6]
    mid_ref, left_ref, right_ref, patch_ref, w_ref, e_ref, w_sem, p_sem = refs[6:]
    pixels, chans = x_ref.shape
    load = pltpu.make_async_copy(w_hbm, w_ref, w_sem)
    load.start()
    amat = amat_ref[...]
    norm_stats(t_ref, nb, amat, get_stats(rp_ref, HALO), get_stats(rn_ref, HALO), stat_ref)
    gain, bias = gain_ref[...], bias_ref[...]

    def act(x, k):
        mean, inv = block_stats(stat_ref, nb, k)
        return silu((x - mean) * (inv * gain) + bias).astype(bf16).astype(f32)

    mid_ref[8 : 8 + HALO, :] = act(rp_ref[0:HALO, :], 0)
    mid_ref[8 + HALO + pixels : 8 + 2 * HALO + pixels, :] = act(rn_ref[0:HALO, :], nb - 1)
    for k in range(nb):
        mid_ref[8 + HALO + k * BLK : 8 + HALO + (k + 1) * BLK, :] = act(x_ref[k * BLK : (k + 1) * BLK, :], k)
    shift_columns(mid_ref, left_ref, right_ref, pixels + 2 * HALO)
    saves = []
    for c in range(0, pixels, CHUNK):
        for k in range(c // BLK, (c + CHUNK) // BLK):
            make_patch((left_ref, mid_ref, right_ref), patch_ref, mask_ref, ints_ref, k, chans)
        save = pltpu.make_async_copy(
            patch_ref.at[pl.ds(c, CHUNK), :], patch_hbm.at[pl.ds(c, CHUNK), :], p_sem.at[c // CHUNK]
        )
        save.start()
        saves.append(save)
        if c == 0:
            load.wait()
        out = dot_nn(patch_ref[c : c + CHUNK, :], w_ref[...]) + cb_ref[...]
        if last:
            out = out + resid_ref[c : c + CHUNK, :]
        out_ref[c : c + CHUNK, :] = out
        for k in range(c // BLK, (c + CHUNK) // BLK):
            x = out_ref[k * BLK : (k + 1) * BLK, :]
            set_sums(e_ref, nb, k, x, x * x)
    own_totals(e_ref, nb, amat, to_ref)
    if last:
        msgp_ref[0:pixels, :] = out_ref[...].astype(bf16)
        msgn_ref[0:pixels, :] = out_ref[...].astype(bf16)
        msgp_ref[pixels : pixels + HALO, :] = cot_ref[0:HALO, :]
        msgn_ref[pixels : pixels + HALO, :] = cot_ref[pixels - HALO : pixels, :]
        at = pixels + HALO
        msgp_ref[at : at + STAT, :] = pack_stats(to_ref[0:1, :], to_ref[nb : nb + 1, :])
        msgn_ref[at : at + STAT, :] = pack_stats(to_ref[nb - 1 : nb, :], to_ref[2 * nb - 1 : 2 * nb, :])
    else:
        send_rows(out_ref, to_ref, nb, msgp_ref, msgn_ref)
    for save in saves:
        save.wait()


def conv_scratch(pixels, chans, nb, w_shape):
    rows = pixels + 2 * HALO + 16
    return [
        pltpu.VMEM((rows, chans), f32),
        pltpu.VMEM((rows, chans), f32),
        pltpu.VMEM((rows, chans), f32),
        pltpu.VMEM((pixels, 9 * chans), bf16),
        pltpu.VMEM(w_shape, bf16),
        pltpu.VMEM((2 * nb, chans), f32),
    ]


def conv_forward(x, recv_p, recv_n, t, amat, gain, bias, mask, ints, weight, cb, resid=None, cot=None):
    pixels, chans = x.shape
    nb = pixels // BLK
    last = resid is not None
    msg = sds((pixels + HALO + STAT, chans), bf16) if last else sds((HALO + 8, chans), f32)
    operands = [x, recv_p, recv_n, t, amat, gain, bias, mask, ints, weight.reshape(9 * chans, chans), cb]
    ins = [VM, VM, VM, VM, VM, VM, VM, VM, SM, HB, VM]
    if last:
        operands += [resid, cot]
        ins += [VM, VM]
    stats = sds((2 * nb, chans), f32)
    outs = [(sds((pixels, chans), f32), VM), (stats, VM), (stats, VM), (msg, VM), (msg, VM)]
    outs.append((sds((pixels, 9 * chans), bf16), HB))
    scratch = conv_scratch(pixels, chans, nb, (9 * chans, chans))
    scratch += [pltpu.SemaphoreType.DMA, pltpu.SemaphoreType.DMA((pixels // CHUNK,))]
    flops = 18 * pixels * chans * chans
    return call(functools.partial(conv_forward_kernel, nb, last), ins, outs, scratch, operands, flops)


def attention_kernel(nb, *refs):
    (
        x_ref, rp_ref, rn_ref, t_ref, amat_ref, gain_ref, bias_ref, ints_ref, img_ref,
        wq_ref, wk_ref, wv_ref, wp_ref, bq_ref, bv_ref, bp_ref, cot_ref,
    ) = refs[:17]
    (
        norm_hbm, dk_hbm, dv_hbm, out_ref, attn_ref, dq_ref, u_ref, stat_ref, to_ref, vec_ref, msgp_ref, msgn_ref,
    ) = refs[17:29]
    norm_ref, dk_ref, dv_ref, q_ref, k_ref, v_ref, da_ref, at_ref, dqf_ref, dkf_ref, dvf_ref, e_ref, h_ref, sems = refs[29:]
    pixels, chans = x_ref.shape
    own = pixels // CHUNK
    scale = 1.0 / math.sqrt(chans)
    amat = amat_ref[...]
    at = pixels + HALO
    prev_stats = unpack_stats(rp_ref[at : at + STAT, :])
    next_stats = unpack_stats(rn_ref[at : at + STAT, :])
    norm_stats(t_ref, nb, amat, prev_stats, next_stats, stat_ref)
    gain, bias = gain_ref[...], bias_ref[...]
    chunk_lo = ints_ref[1, 0] // CHUNK
    chunk_hi = (ints_ref[2, nb - 1] + CHUNK - 1) // CHUNK
    copies = []

    def send(scratch, hbm, which, c):
        r = pl.ds(c * CHUNK, CHUNK)
        copy = pltpu.make_async_copy(scratch.at[r, :], hbm.at[r, :], sems.at[which, c])
        copy.start()
        copies.append(copy)

    def xhat(c, b):
        r = (c % own) * CHUNK + b * BLK
        if c < own:
            x, k = rp_ref[r : r + BLK, :].astype(f32), 0
        elif c < 2 * own:
            x, k = x_ref[r : r + BLK, :], r // BLK
        else:
            x, k = rn_ref[r : r + BLK, :].astype(f32), nb - 1
        mean, inv = block_stats(stat_ref, nb, k)
        return (x - mean) * inv

    def reached(c, work, otherwise):
        if own <= c < 2 * own:
            work()
        else:
            inside = (c >= chunk_lo) & (c < chunk_hi)
            pl.when(inside)(work)
            pl.when(jnp.logical_not(inside))(otherwise)

    for c in range(3 * own):
        r = slice(c * CHUNK, (c + 1) * CHUNK)

        def keys(c=c, r=r):
            for b in range(CHUNK // BLK):
                norm_ref[c * CHUNK + b * BLK : c * CHUNK + (b + 1) * BLK, :] = (xhat(c, b) * gain + bias).astype(bf16)
            normed = norm_ref[r, :]
            k_ref[r, :] = dot_nn(normed, wk_ref[...]).astype(bf16)
            v_ref[r, :] = (dot_nn(normed, wv_ref[...]) + bv_ref[...]).astype(bf16)
            dkf_ref[r, :] = jnp.zeros((CHUNK, chans), f32)
            dvf_ref[r, :] = jnp.zeros((CHUNK, chans), f32)
            if own <= c < 2 * own:
                o = slice((c - own) * CHUNK, (c - own + 1) * CHUNK)
                q_ref[o, :] = (dot_nn(normed, wq_ref[...]) + bq_ref[...]).astype(bf16)
                da_ref[o, :] = dot_nt(cot_ref[o, :], wp_ref[...]).astype(bf16)

        def nothing(r=r):
            norm_ref[r, :] = jnp.zeros((CHUNK, chans), bf16)

        reached(c, keys, nothing)
        send(norm_ref, norm_hbm, 0, c)
    q_ref[pixels : pixels + CHUNK, :] = jnp.zeros((CHUNK, chans), bf16)
    da_ref[pixels : pixels + CHUNK, :] = jnp.zeros((CHUNK, chans), bf16)

    def attend(count, key_at, row_at, row_end):
        rows = pl.ds(pl.multiple_of(row_at, BLK), CHUNK)
        cols = pl.ds(pl.multiple_of(key_at, BLK), count)
        s = dot_nt(q_ref[rows, :], k_ref[cols, :]) * scale
        p = jnp.exp(s - jnp.max(s, axis=1, keepdims=True))
        at_row = lax.broadcasted_iota(jnp.int32, (CHUNK, 1), 0) + row_at
        p = p * jnp.where(at_row < row_end, 1.0 / jnp.sum(p, axis=1, keepdims=True), 0.0)
        low = p.astype(bf16)
        d_attn = da_ref[rows, :]
        dp = dot_nt(d_attn, v_ref[cols, :])
        at_ref[rows, :] = dot_nn(low, v_ref[cols, :]).astype(bf16)
        dvf_ref[cols, :] += dot_tn(low, d_attn)
        ds = (p * (dp - jnp.sum(p * dp, axis=1, keepdims=True))).astype(bf16)
        dqf_ref[rows, :] = (dot_nn(ds, k_ref[cols, :]) * scale).astype(bf16)
        dkf_ref[cols, :] += dot_tn(ds, q_ref[rows, :])

    def image(m, carry):
        key_at, side, begin, end = (img_ref[t, m] for t in range(4))
        for kind in (GRID // 2, 3 * GRID // 4, GRID):

            @pl.when(side == kind)
            def _():
                def block(i, inner):
                    attend(kind * kind, key_at, begin + i * CHUNK, end)
                    return inner

                lax.fori_loop(0, (end - begin + CHUNK - 1) // CHUNK, block, 0)

        return carry

    lax.fori_loop(0, img_ref[4, 0], image, 0)
    h_ref[...] = jnp.zeros(h_ref.shape, f32)
    for c in range(3 * own):
        r = slice(c * CHUNK, (c + 1) * CHUNK)
        o = slice((c % own) * CHUNK, (c % own + 1) * CHUNK)

        def fold(c=c, r=r, o=o):
            d_key = (dkf_ref[r, :] * scale).astype(bf16)
            d_value = dvf_ref[r, :].astype(bf16)
            dk_ref[r, :] = d_key
            dv_ref[r, :] = d_value
            u = dot_nt(d_key, wk_ref[...]) + dot_nt(d_value, wv_ref[...])
            if own <= c < 2 * own:
                d_query = dqf_ref[o, :]
                dq_ref[o, :] = d_query
                attn = at_ref[o, :]
                attn_ref[o, :] = attn
                out_ref[o, :] = (x_ref[o, :] + dot_nn(attn, wp_ref[...]) + bp_ref[...]).astype(bf16)
                u_ref[o, :] = u + dot_nt(d_query, wq_ref[...])
                for b in range(CHUNK // BLK):
                    k = (c - own) * (CHUNK // BLK) + b
                    u = u_ref[k * BLK : (k + 1) * BLK, :]
                    set_sums(e_ref, nb, k, u, u * xhat(c, b))
            else:
                msg_ref, row = (msgp_ref, 0) if c < own else (msgn_ref, 2)
                msg_ref[o, :] = u.astype(bf16)
                for b in range(CHUNK // BLK):
                    part = u[b * BLK : (b + 1) * BLK, :]
                    h_ref[row : row + 1, :] += jnp.sum(part, axis=0, keepdims=True)
                    h_ref[row + 1 : row + 2, :] += jnp.sum(part * xhat(c, b), axis=0, keepdims=True)

        def nothing(c=c, r=r, o=o):
            zero = jnp.zeros((CHUNK, chans), bf16)
            dk_ref[r, :] = zero
            dv_ref[r, :] = zero
            (msgp_ref if c < own else msgn_ref)[o, :] = zero

        reached(c, fold, nothing)
        send(dk_ref, dk_hbm, 1, c)
        send(dv_ref, dv_hbm, 2, c)
    before, before_x, after, after_x = (h_ref[i : i + 1, :] for i in range(4))
    d_bias = jnp.sum(e_ref[0:nb, :], axis=0, keepdims=True) + before + after
    d_gain = jnp.sum(e_ref[nb : 2 * nb, :], axis=0, keepdims=True) + before_x + after_x
    vec_ref[...] = stat_rows(d_gain, d_bias)
    e_ref[0:1, :] += before
    e_ref[nb : nb + 1, :] += before_x
    e_ref[nb - 1 : nb, :] += after
    e_ref[2 * nb - 1 : 2 * nb, :] += after_x
    e_ref[...] = e_ref[...] * gain
    own_totals(e_ref, nb, amat, to_ref)
    msgp_ref[pixels : pixels + HALO, :] = u_ref[0:HALO, :].astype(bf16)
    msgn_ref[pixels : pixels + HALO, :] = u_ref[pixels - HALO : pixels, :].astype(bf16)
    msgp_ref[at : at + STAT, :] = pack_stats(to_ref[0:1, :], to_ref[nb : nb + 1, :])
    msgn_ref[at : at + STAT, :] = pack_stats(to_ref[nb - 1 : nb, :], to_ref[2 * nb - 1 : 2 * nb, :])
    for copy in copies:
        copy.wait()


def attention(x, recv_p, recv_n, t, amat, gain, bias, ints, images, wq, wk, wv, wp, bq, bv, bp, cot):
    pixels, chans = x.shape
    nb, ext = pixels // BLK, 3 * pixels
    rows16, rows32 = sds((pixels, chans), bf16), sds((pixels, chans), f32)
    ext16 = sds((ext, chans), bf16)
    stats = sds((2 * nb, chans), f32)
    msg = sds((pixels + HALO + STAT, chans), bf16)
    outs = [(ext16, HB)] * 3
    outs += [(o, VM) for o in (rows16, rows16, rows16, rows32, stats, stats, sds((8, chans), f32), msg, msg)]
    padded = pltpu.VMEM((pixels + CHUNK, chans), bf16)
    window = pltpu.VMEM((ext, chans), bf16)
    wide = pltpu.VMEM((ext, chans), f32)
    scratch = [window, window, window, padded, window, window, padded, padded, padded, wide, wide]
    scratch += [pltpu.VMEM((2 * nb, chans), f32), pltpu.VMEM((8, chans), f32)]
    scratch.append(pltpu.SemaphoreType.DMA((3, ext // CHUNK)))
    ins = [VM] * 7 + [SM, SM] + [VM] * 8
    operands = (x, recv_p, recv_n, t, amat, gain, bias, ints, images, wq, wk, wv, wp, bq, bv, bp, cot)
    flops = 2 * pixels * chans * (chans * 9 + 6 * 1280)
    return call(functools.partial(attention_kernel, nb), ins, outs, scratch, operands, flops)


def conv_backward_kernel(nb, first, *refs):
    refs = refs[1:]
    if first:
        u_ref, mine_p_ref, mine_n_ref, rp_ref, rn_ref, xp_ref, xn_ref, cot_ref = refs[:8]
        refs = refs[8:]
    else:
        u_ref, rp_ref, rn_ref, xp_ref, xn_ref = refs[:5]
        refs = refs[5:]
    x_ref, stat_ref, s_ref, gain_ref, amat_ref, mask_ref, ints_ref, w_hbm = refs[:8]
    y_ref, ystat_ref, ygain_ref, ybias_ref = refs[8:12]
    refs = refs[12:]
    if first:
        mid_out_ref, refs = refs[0], refs[1:]
    err_ref, v_ref, so_ref, vec_ref, msgp_ref, msgn_ref = refs[:6]
    mid_ref, left_ref, right_ref, patch_ref, w_ref, e_ref, w_sem = refs[6:]
    pixels, chans = x_ref.shape
    loads = []
    for tap in range(9):
        load = pltpu.make_async_copy(
            w_hbm.at[8 - tap], w_ref.at[:, pl.ds(tap * chans, chans)], w_sem.at[tap]
        )
        load.start()
        loads.append(load)
    amat = amat_ref[...]
    if first:
        at = pixels + HALO
        prev_stats = unpack_stats(rp_ref[at : at + STAT, :])
        next_stats = unpack_stats(rn_ref[at : at + STAT, :])
    else:
        prev_stats, next_stats = get_stats(rp_ref, HALO), get_stats(rn_ref, HALO)
    one, two = totals(s_ref, nb, amat, prev_stats, next_stats)
    e_ref[0:nb, :] = one
    e_ref[nb : 2 * nb, :] = two
    gain = gain_ref[...]

    def grad(u, x, k):
        mean, inv = block_stats(stat_ref, nb, k)
        m_one, m_two = block_stats(e_ref, nb, k)
        return inv * (u * gain - m_one - (x - mean) * inv * m_two)

    if first:
        low, high = slice(pixels - HALO, pixels), slice(0, HALO)
        side = slice(pixels, pixels + HALO)
        u = mine_p_ref[low, :].astype(f32) + rp_ref[side, :].astype(f32)
        before = xp_ref[side, :].astype(f32) + grad(u, xp_ref[low, :].astype(f32), 0)
        u = mine_n_ref[high, :].astype(f32) + rn_ref[side, :].astype(f32)
        after = xn_ref[side, :].astype(f32) + grad(u, xn_ref[high, :].astype(f32), nb - 1)
    else:
        before = grad(rp_ref[0:HALO, :], xp_ref[0:HALO, :], 0)
        after = grad(rn_ref[0:HALO, :], xn_ref[0:HALO, :], nb - 1)
    mid_ref[8 : 8 + HALO, :] = before.astype(bf16).astype(f32)
    mid_ref[8 + HALO + pixels : 8 + 2 * HALO + pixels, :] = after.astype(bf16).astype(f32)
    column = jnp.zeros((1, chans), f32)
    for k in range(nb):
        r = slice(k * BLK, (k + 1) * BLK)
        u = u_ref[r, :]
        if first:
            u = u + rp_ref[r, :].astype(f32) + rn_ref[r, :].astype(f32)
        g = grad(u, x_ref[r, :], k)
        if first:
            g = g + cot_ref[r, :].astype(f32)
            mid_out_ref[r, :] = g
        low = g.astype(bf16)
        err_ref[r, :] = low
        g = low.astype(f32)
        column = column + jnp.sum(g, axis=0, keepdims=True)
        mid_ref[8 + HALO + k * BLK : 8 + HALO + (k + 1) * BLK, :] = g
    shift_columns(mid_ref, left_ref, right_ref, pixels + 2 * HALO)
    y_gain, y_bias = ygain_ref[...], ybias_ref[...]
    for c in range(0, pixels, CHUNK):
        for k in range(c // BLK, (c + CHUNK) // BLK):
            make_patch((left_ref, mid_ref, right_ref), patch_ref, mask_ref, ints_ref, k, chans)
        if c == 0:
            for load in loads:
                load.wait()
        v_ref[c : c + CHUNK, :] = dot_nt(patch_ref[c : c + CHUNK, :], w_ref[...])
        for k in range(c // BLK, (c + CHUNK) // BLK):
            r = slice(k * BLK, (k + 1) * BLK)
            mean, inv = block_stats(ystat_ref, nb, k)
            xh = (y_ref[r, :] - mean) * inv
            v = v_ref[r, :] * silu_slope(xh * y_gain + y_bias)
            v_ref[r, :] = v
            set_sums(e_ref, nb, k, v, v * xh)
    d_bias = jnp.sum(e_ref[0:nb, :], axis=0, keepdims=True)
    d_gain = jnp.sum(e_ref[nb : 2 * nb, :], axis=0, keepdims=True)
    vec_ref[...] = jnp.concatenate([d_gain, d_bias, column, jnp.zeros((5, chans), f32)], axis=0)
    e_ref[...] = e_ref[...] * y_gain
    own_totals(e_ref, nb, amat, so_ref)
    if first:
        send_rows(v_ref, so_ref, nb, msgp_ref, msgn_ref)
    else:
        send_stats(so_ref, nb, msgp_ref, msgn_ref, 0)


def conv_backward(first, token, heads, x, stat, s, gain, amat, mask, ints, weight, y, ystat, ygain, ybias):
    pixels, chans = x.shape
    nb = pixels // BLK
    operands = [token, *heads, x, stat, s, gain, amat, mask, ints, weight.reshape(9, chans, chans), y, ystat, ygain, ybias]
    ins = [HB] + [VM] * len(heads) + [VM] * 6 + [SM, HB] + [VM] * 4
    msg = sds((HALO + 8 if first else 8, chans), f32)
    rows = sds((pixels, chans), f32)
    outs = [rows] if first else []
    outs += [sds((pixels, chans), bf16), rows, sds((2 * nb, chans), f32), sds((8, chans), f32), msg, msg]
    scratch = conv_scratch(pixels, chans, nb, (chans, 9 * chans)) + [pltpu.SemaphoreType.DMA((9,))]
    flops = 18 * pixels * chans * chans
    return call(
        functools.partial(conv_backward_kernel, nb, first), ins, [(o, VM) for o in outs], scratch, operands, flops
    )


def tail_kernel(nb, passes, *refs):
    v_ref, rp_ref, rn_ref, s_ref, x_ref, stat_ref, gain_ref, amat_ref, mid_ref, w_ref = refs[passes : passes + 10]
    err_ref, fg_ref, vec_ref, e_ref = refs[2 * passes + 10 :]
    pixels, chans = x_ref.shape
    one, two = totals(s_ref, nb, amat_ref[...], get_stats(rp_ref, 0), get_stats(rn_ref, 0))
    e_ref[0:nb, :] = one
    e_ref[nb : 2 * nb, :] = two
    gain = gain_ref[...]
    column = jnp.zeros((1, chans), f32)
    for c in range(0, pixels, CHUNK):
        for k in range(c // BLK, (c + CHUNK) // BLK):
            r = slice(k * BLK, (k + 1) * BLK)
            mean, inv = block_stats(stat_ref, nb, k)
            m_one, m_two = block_stats(e_ref, nb, k)
            g = mid_ref[r, :] + inv * (v_ref[r, :] * gain - m_one - (x_ref[r, :] - mean) * inv * m_two)
            low = g.astype(bf16)
            err_ref[r, :] = low
            column = column + jnp.sum(low.astype(f32), axis=0, keepdims=True)
        fg_ref[c : c + CHUNK, :] = dot_nt(err_ref[c : c + CHUNK, :], w_ref[...]).astype(bf16)
    vec_ref[...] = jnp.concatenate([column, jnp.zeros((7, chans), f32)], axis=0)


def tail(passed, v, recv_p, recv_n, s, x, stat, gain, amat, mid, w_in):
    pixels, chans = x.shape
    nb = pixels // BLK
    count = len(passed)
    outs = [(sds(a.shape, a.dtype), HB) for a in passed]
    outs += [(sds((pixels, chans), bf16), VM), (sds((pixels, w_in.shape[0]), bf16), VM), (sds((8, chans), f32), VM)]
    operands = (*passed, v, recv_p, recv_n, s, x, stat, gain, amat, mid, w_in)
    scratch = [pltpu.VMEM((2 * nb, chans), f32)]
    flops = 2 * pixels * chans * w_in.shape[0]
    body = functools.partial(tail_kernel, nb, count)
    aliases = {i: i for i in range(count)}
    return call(body, [HB] * count + [VM] * 10, outs, scratch, operands, flops, aliases=aliases)


def finish_kernel(places, tokens, *refs):
    up_ref, mine_hbm, other_hbm, *out_refs, read_ref, stage_ref, read_sems, sems = refs[tokens:]
    slots = stage_ref.shape[0]

    def write(own):
        work = []
        for source, half in ((mine_hbm, own), (other_hbm, 1 - own)):
            for row, moves in places(half, out_refs):
                work.append((source.at[pl.ds(row, CHUNK), :], moves))
        reads = [
            pltpu.make_async_copy(source, read_ref.at[i % slots], read_sems.at[i % slots])
            for i, (source, _) in enumerate(work)
        ]
        for read in reads[:slots]:
            read.start()
        pending = [[] for _ in range(slots)]
        for i, (_, moves) in enumerate(work):
            slot = i % slots
            reads[i].wait()
            for copy in pending[slot]:
                copy.wait()
            stage_ref[slot] = read_ref[slot].astype(f32)
            if i + slots < len(work):
                reads[i + slots].start()
            pending[slot] = []
            for k, (lanes, target) in enumerate(moves):
                copy = pltpu.make_async_copy(stage_ref.at[slot, :, lanes], target, sems.at[slot, k])
                copy.start()
                pending[slot].append(copy)
        for copies in pending:
            for copy in copies:
                copy.wait()

    for own in range(2):
        pl.when(up_ref[0] == own)(functools.partial(write, own))


def finish(places, up, mine, outs, tokens=()):
    chans = mine.shape[1]
    slots = 16
    scratch = [pltpu.VMEM((slots, CHUNK, chans), bf16), pltpu.VMEM((slots, CHUNK, chans), f32)]
    scratch += [pltpu.SemaphoreType.DMA((slots,)), pltpu.SemaphoreType.DMA((slots, 2))]
    body = functools.partial(finish_kernel, places, len(tokens))
    operands = (*tokens, up.reshape(1), mine, partner(mine, "rows", 1))
    return call(body, [HB] * len(tokens) + [SM, HB, HB], [(o, HB) for o in outs], scratch, operands, 0)


def conv_places(half, out_ref):
    rows = out_ref.shape[0] // 2
    return [(r, [(slice(None), out_ref.at[pl.ds(half * rows + r, CHUNK), :])]) for r in range(0, rows, CHUNK)]


def early_places(half, out_refs):
    conv_ref, *squares = out_refs
    out = conv_places(half, conv_ref)
    row = conv_ref.shape[0] // 2
    for ref in squares[2 * half : 2 * half + 2]:
        for r in range(0, ref.shape[0], CHUNK):
            out.append((row, [(slice(None), ref.at[pl.ds(r, CHUNK), :])]))
            row += CHUNK
    return out


def late_places(half, out_refs):
    conv_ref, in_ref, vec_ref = out_refs
    return conv_places(half, conv_ref) + [(conv_ref.shape[0] // 2, [(slice(None), (in_ref, vec_ref)[half])])]


def book_places(half, out_refs):
    (book_ref,) = out_refs
    quarter, emb = book_ref.shape[0] // 4, book_ref.shape[1]
    out = []
    for r in range(0, quarter, CHUNK):
        to = half * quarter + r
        left = (pl.ds(0, emb), book_ref.at[pl.ds(to, CHUNK), :])
        right = (pl.ds(emb, emb), book_ref.at[pl.ds(2 * quarter + to, CHUNK), :])
        out.append((r, [left, right]))
    return out


def gate_kernel(*refs):
    pass


def gate(passed, *tokens):
    outs = [(sds(passed.shape, passed.dtype), HB)]
    return call(gate_kernel, [HB] * (1 + len(tokens)), outs, [], (passed, *tokens), 0, aliases={0: 0}, light=True)[0]


def along(array, axis, by):
    count = lax.axis_size(axis)
    return lax.ppermute(array, axis, [(i, i + by) for i in range(count) if 0 <= i + by < count])


def around(array, axis, by):
    count = lax.axis_size(axis)
    return lax.ppermute(array, axis, [(i, (i + by) % count) for i in range(count)])


def swap(to_prev, to_next):
    return along(to_next, "rows", 1), along(to_prev, "rows", -1)


def partner(array, axis, bit):
    return lax.ppermute(array, axis, [(i, i ^ bit) for i in range(lax.axis_size(axis))])


def bits(axis):
    return [(axis, 1 << b) for b in range(lax.axis_size(axis).bit_length() - 1)]


def half_of(x, which):
    return lax.dynamic_slice_in_dim(x, which * (x.shape[0] // 2), x.shape[0] // 2)


def core_send(arrays):
    up = lax.axis_index("rows") % 2
    send = [half_of(x, 1 - up) for x in arrays]
    return partner(jnp.concatenate(send) if len(send) > 1 else send[0], "rows", 1)


def add(one, two):
    return (one.astype(f32) + two.astype(f32)).astype(bf16)


def join(parts):
    return jnp.concatenate(parts) if len(parts) > 1 else parts[0]


def exchange(axis, bit, jobs):
    up = (lax.axis_index(axis) // bit) % 2
    keep = [half_of(x, up) if reduce else x for reduce, x in jobs]
    got = partner(join([half_of(x, 1 - up) if reduce else x for reduce, x in jobs]), axis, bit)
    at, out = 0, []
    for (reduce, _), x in zip(jobs, keep):
        other = got[at : at + x.shape[0]]
        at += x.shape[0]
        if reduce:
            out.append(add(x, other))
        else:
            out.append(jnp.where(up == 0, jnp.concatenate([x, other]), jnp.concatenate([other, x])))
    return out


def plan(flip, *axes):
    middle = bits(axes[0])[1:]
    steps = (middle[::-1] if flip else middle) + [step for axis in axes[1:] for step in bits(axis)]
    return [(step, True) for step in steps] + [(step, False) for step in steps[::-1]]


def rounds(arrays, plans, begins, turns=None):
    arrays = list(arrays)
    for turn in turns or range(max(begin + len(p) for p, begin in zip(plans, begins))):
        by_partner = {}
        for i, (p, begin) in enumerate(zip(plans, begins)):
            if 0 <= turn - begin < len(p):
                step, reduce = p[turn - begin]
                by_partner.setdefault((begin, *step), []).append((i, reduce))
        for (_, *step), jobs in by_partner.items():
            out = exchange(*step, [(reduce, arrays[i]) for i, reduce in jobs])
            for (i, _), x in zip(jobs, out):
                arrays[i] = x
    return arrays


def streams(x, *axes):
    world = math.prod(lax.axis_size(axis) for axis in axes) // 2
    unit = 16 * world
    cut = -(-x.shape[0] // (2 * unit)) * unit
    return [x[:cut], x[cut:]]


def half_of(x, which):
    return lax.dynamic_slice_in_dim(x, which * (x.shape[0] // 2), x.shape[0] // 2)


def core_send(x):
    return partner(half_of(x, 1 - lax.axis_index("rows") % 2), "rows", 1)


def core_half(x):
    return half_of(x, lax.axis_index("rows") % 2)


def core_swap(x):
    return core_half(x), core_send(x)


def per_device(
    features, indices, img_width, img_start, codebook, w_in, b_in, gn1_gain, gn1_bias, conv1_w, conv1_b,
    gn2_gain, gn2_bias, conv2_w, conv2_b, gn3_gain, gn3_bias, w_query, b_query, w_key, w_value, b_value,
    w_proj, b_proj, cotangent,
):
    pixels, emb = features.shape[1], features.shape[2]
    chans = w_in.shape[1]
    nb = pixels // BLK
    widths, starts = img_width[0], img_start[0]
    first_pos = lax.axis_index("rows") * pixels
    row = lambda v: v.reshape(1, -1)

    positions = first_pos + jnp.arange(pixels, dtype=jnp.int32)
    image_id = jnp.sum((starts[None, :] <= positions[:, None]).astype(jnp.int32), axis=1) - 1
    choose = image_id[:, None] == jnp.arange(widths.shape[0], dtype=jnp.int32)[None, :]
    side = jnp.sum(jnp.where(choose, widths[None, :], 0), axis=1)
    begin = jnp.sum(jnp.where(choose, starts[None, :], 0), axis=1)
    offset = positions - begin
    safe = jnp.maximum(side, 1)
    row_at, col_at = offset // safe, offset % safe
    valid = []
    for dr in (-1, 0, 1):
        for dc in (-1, 0, 1):
            r, c = row_at + dr, col_at + dc
            valid.append((r >= 0) & (r < side) & (c >= 0) & (c < side))
    mask = jnp.stack(valid, axis=1).astype(f32)
    low_key = begin - first_pos + pixels
    spans = jnp.stack([low_key, low_key + side * side], axis=1)
    block_id = image_id[::BLK]
    ints = jnp.stack([side[::BLK], spans[::BLK, 0], spans[::BLK, 1]])
    count = (jnp.maximum(side * side, 1)[::BLK] * (chans // GN_GROUPS)).astype(f32)
    amat = jnp.concatenate(
        [
            (block_id[:, None] == block_id[None, :]).astype(f32),
            (block_id == block_id[0]).astype(f32)[:, None],
            (block_id == block_id[-1]).astype(f32)[:, None],
            (1.0 / count)[:, None],
        ],
        axis=1,
    )

    at_image = jnp.minimum(block_id[0] + jnp.arange(8, dtype=jnp.int32), widths.shape[0] - 1)
    pick = at_image[:, None] == jnp.arange(widths.shape[0], dtype=jnp.int32)[None, :]
    img_side = jnp.sum(jnp.where(pick, widths[None, :], 0), axis=1)
    img_at = jnp.sum(jnp.where(pick, starts[None, :], 0), axis=1) - first_pos
    images = jnp.stack(
        [
            img_at + pixels,
            img_side,
            jnp.maximum(img_at, 0),
            jnp.minimum(img_at + img_side * img_side, pixels),
            jnp.broadcast_to(block_id[-1] - block_id[0] + 1, (8,)),
        ]
    )

    groups = lax.axis_size("chan")
    codes = codebook.shape[0]
    ring = [indices[0]] + [around(indices, "chan", -d)[0] for d in range(1, groups)]
    local = [index - lax.axis_index("chan") * codes for index in ring]
    found = [lookup(index[:, None], codebook) for index in local[1:]]
    found.insert(0, lookup(local[0][:, None], codebook, found))
    rows_in = [found[0]] + [around(found[d], "chan", d) for d in range(1, groups)]

    stats2 = sds((2 * nb, chans), f32)
    rows32 = sds((pixels, chans), f32)
    msg32 = sds((HALO + 8, chans), f32)
    quant, resid_in, t_one, to_p, to_n = call(
        functools.partial(lift_kernel, groups, nb),
        [VM] * (4 + groups),
        [(o, VM) for o in (sds((pixels, emb), bf16), rows32, stats2, msg32, msg32)],
        [pltpu.VMEM((2 * nb, chans), f32)],
        (features[0], *rows_in, w_in, row(b_in), amat),
        2 * pixels * emb * chans,
    )
    p_one, n_one = swap(to_p, to_n)
    hid_one, stat_one, t_two, to_p, to_n, patch_one = conv_forward(
        resid_in, p_one, n_one, t_one, amat, row(gn1_gain), row(gn1_bias), mask, ints, conv1_w, row(conv1_b)
    )
    p_two, n_two = swap(to_p, to_n)
    cot = cotangent[0]
    resid_mid, stat_two, t_three, to_p, to_n, patch_two = conv_forward(
        hid_one, p_two, n_two, t_two, amat, row(gn2_gain), row(gn2_bias), mask, ints, conv2_w, row(conv2_b),
        resid_in, cot,
    )
    p_three, n_three = swap(to_p, to_n)
    normed, d_key, d_value, output, attn, d_query, u_own, stat_three, s_three, vec_three, to_p, to_n = attention(
        resid_mid, p_three, n_three, t_three, amat, row(gn3_gain), row(gn3_bias), ints, images,
        w_query, w_key, w_value, w_proj, row(b_query), row(b_value), row(b_proj), cot,
    )
    p_back, n_back = swap(to_p, to_n)
    tn = lambda a, b: jnp.einsum("nk,nc->kc", a, b, preferred_element_type=f32).astype(bf16)
    own_normed = normed[pixels : 2 * pixels]
    g_proj = tn(attn, cot)
    g_query = tn(own_normed, d_query)
    g_key = tn(normed, d_key)
    g_value = tn(normed, d_value)
    g_attn = jnp.concatenate([g_proj, g_query, g_key, g_value])
    g_b_proj = jnp.sum(cot.astype(f32), axis=0, keepdims=True)
    g_b_query = jnp.sum(d_query.astype(f32), axis=0, keepdims=True)
    g_b_value = jnp.sum(d_value.astype(f32), axis=0, keepdims=True)
    d_mid, err_two, v_two, s_two, vec_two, msg_p, msg_n = conv_backward(
        True, g_attn, (u_own, to_p, to_n, p_back, n_back, p_three, n_three, cot),
        resid_mid, stat_three, s_three, row(gn3_gain), amat, mask, ints, conv2_w,
        hid_one, stat_two, row(gn2_gain), row(gn2_bias),
    )
    p_four, n_four = swap(msg_p, msg_n)
    g_conv2 = tn(patch_two, err_two)
    two_got, attn_got = core_send(g_conv2), core_send(g_attn)
    err_one, v_one, s_one, vec_one, msg_p, msg_n = conv_backward(
        False, g_conv2, (v_two, p_four, n_four, p_two, n_two),
        hid_one, stat_two, s_two, row(gn2_gain), amat, mask, ints, conv1_w,
        resid_in, stat_one, row(gn1_gain), row(gn1_bias),
    )
    p_five, n_five = swap(msg_p, msg_n)
    err_one, two_got, attn_got, err_in, feature_grad, vec_in = tail(
        (err_one, two_got, attn_got), v_one, p_five, n_five, s_one, resid_in, stat_one, row(gn1_gain), amat, d_mid, w_in
    )
    below, above = [feature_grad], [feature_grad]
    for _ in range(1, groups):
        below.append(along(below[-1], "chan", 1))
        above.append(along(above[-1], "chan", -1))
    two = jnp.concatenate([add(core_half(g_conv2), two_got), add(core_half(g_attn), attn_got)])
    g_conv1 = tn(patch_one, gate(err_one, two))
    vectors = (vec_in, vec_one, vec_two, vec_three, g_b_query, g_b_value, g_b_proj)
    both = [plan(flip, "rows", "chan") for flip in (False, True)]
    plans = both + both + both[1:] + [plan(flip, "rows") for flip in (False, True)]
    begins = [0, 0, LATE_ROUND, LATE_ROUND, LATE_ROUND, BOOK_ROUND, BOOK_ROUND]
    work = rounds(streams(two, "rows", "chan"), plans[:2], begins, range(1))
    g_conv1, begun, small = own_part(g_conv1, work[0], row(local[0]), feature_grad, quant, err_in, vectors, codes)
    one = add(*core_swap(g_conv1))
    small = add(*core_swap(small))
    pair = lambda d: (row(local[groups - d]), (below[d], above[groups - d]))
    middle = [pair(d) for d in range(1, groups) if 2 * d == groups]
    outer = [pair(d) for d in range(1, groups) if 2 * d != groups]
    book = scatter(*zip(*middle), codes, f32, begun, work)
    work = rounds(work, plans[:2], begins, range(1, 2))
    book = scatter(*zip(*outer), codes, bf16, book, work)
    book = add(*core_swap(book))
    work += streams(one, "rows", "chan") + [small] + streams(book, "rows")
    turns = max(begin + len(p) for p, begin in zip(plans, begins))
    work = rounds(work, plans, begins, range(2, turns))
    up = lax.axis_index("rows") % 2
    square, conv = sds((chans, chans), f32), sds((9 * chans, chans), f32)
    early = finish(early_places, up, jnp.concatenate(work[:2]), [conv] + [square] * 4)
    book = finish(book_places, up, jnp.concatenate(work[5:]), [sds((codes, emb), f32)])
    narrow = [sds((emb, chans), f32), sds((chans - emb, chans), f32)]
    sum_one, s_in, vec = finish(
        late_places, up, jnp.concatenate(work[2:5]), [conv] + narrow, (early[0], book[0])
    )
    sum_two, s_proj, s_query, s_key, s_value = early
    (book_grad,) = book
    return (
        output[None],
        feature_grad[None],
        book_grad,
        s_in,
        vec[0],
        vec[1],
        vec[2],
        sum_one.reshape(conv1_w.shape),
        vec[3],
        vec[4],
        vec[5],
        sum_two.reshape(conv2_w.shape),
        vec[6],
        vec[7],
        vec[8],
        s_query,
        vec[9],
        s_key,
        s_value,
        vec[10],
        s_proj,
        vec[11],
    )


def solution(mesh):
    group, copied = P("chan", "rows", None), P()
    placed = (group, P("chan", "rows"), P("chan", None), P("chan", None), P("chan", None))
    return jax.shard_map(
        per_device,
        mesh=mesh,
        in_specs=placed + (copied,) * 19 + (group,),
        out_specs=(group, group, P("chan", None)) + (copied,) * 19,
        check_vma=False,
    )
```

```python
import functools
import math

import jax
import jax.numpy as jnp
from jax import lax
from jax.experimental import pallas as pl
from jax.experimental.pallas import tpu as pltpu
from jax.sharding import PartitionSpec as P

GN_GROUPS = 32
GRID = 32
BLK = (GRID // 4) ** 2
HALO = 64
CHUNK = 256
STAT = 16
epsilon = 1e-06
masked_score = -1e30
f32 = jnp.float32
bf16 = jnp.bfloat16
MIB = 1 << 20
LATE_ROUND = 2
BOOK_ROUND = 4

VM = pl.BlockSpec(memory_space=pltpu.VMEM)
SM = pl.BlockSpec(memory_space=pltpu.SMEM)
HB = pl.BlockSpec(memory_space=pl.ANY)


def call(body, ins, outs, scratch, operands, flops, vmem=58, aliases={}, light=False):
    bytes_all = sum(math.prod(a.shape) * a.dtype.itemsize for a in (*operands, *[o[0] for o in outs]))
    if light:
        flops = bytes_all = 0
    return pl.pallas_call(
        body,
        out_shape=[o[0] for o in outs],
        in_specs=ins,
        out_specs=[o[1] for o in outs],
        scratch_shapes=scratch,
        input_output_aliases=aliases,
        compiler_params=pltpu.CompilerParams(vmem_limit_bytes=vmem * MIB),
        cost_estimate=pl.CostEstimate(flops=flops, bytes_accessed=bytes_all, transcendentals=0),
    )(*operands)


def sds(shape, dtype):
    return jax.ShapeDtypeStruct(shape, dtype)


def dot_nn(a, b):
    return lax.dot_general(a, b, (((1,), (0,)), ((), ())), preferred_element_type=f32)


def dot_nt(a, b):
    return lax.dot_general(a, b, (((1,), (1,)), ((), ())), preferred_element_type=f32)


def dot_tn(a, b):
    return lax.dot_general(a, b, (((0,), (0,)), ((), ())), preferred_element_type=f32)


def group_total(x):
    per = x.shape[1] // GN_GROUPS
    lane = lax.broadcasted_iota(jnp.int32, x.shape, 1)
    step = 1
    while step < per:
        up = pltpu.roll(x, step, 1)
        down = pltpu.roll(x, x.shape[1] - step, 1)
        x = x + jnp.where((lane & step) != 0, up, down)
        step *= 2
    return x


def image_total(e_ref, row, nb, amat):
    total = amat[:, 0:1] * e_ref[row : row + 1, :]
    for j in range(1, nb):
        total = total + amat[:, j : j + 1] * e_ref[row + j : row + j + 1, :]
    return total


def split3(v):
    high = v.astype(bf16)
    rest = v - high.astype(f32)
    mid = rest.astype(bf16)
    low = (rest - mid.astype(f32)).astype(bf16)
    return high, mid, low


def pack_stats(a, b):
    rows = [p.astype(f32) for p in (*split3(a), *split3(b))]
    rows.append(jnp.zeros((STAT - 6, a.shape[1]), f32))
    return jnp.concatenate(rows, axis=0).astype(bf16)


def unpack_stats(block):
    v = block.astype(f32)
    return v[0:1] + v[1:2] + v[2:3], v[3:4] + v[4:5] + v[5:6]


def stat_rows(a, b):
    return jnp.concatenate([a, b, jnp.zeros((6, a.shape[1]), f32)], axis=0)


def totals(t_ref, nb, amat, prev_rows, next_rows):
    first, last = amat[:, nb : nb + 1], amat[:, nb + 1 : nb + 2]
    one = t_ref[0:nb, :] + first * prev_rows[0] + last * next_rows[0]
    two = t_ref[nb : 2 * nb, :] + first * prev_rows[1] + last * next_rows[1]
    inv_count = amat[:, nb + 2 : nb + 3]
    return one * inv_count, two * inv_count


def norm_stats(t_ref, nb, amat, prev_rows, next_rows, stat_ref):
    mean, square = totals(t_ref, nb, amat, prev_rows, next_rows)
    stat_ref[0:nb, :] = mean
    stat_ref[nb : 2 * nb, :] = lax.rsqrt(square - mean * mean + epsilon)


def block_stats(stat_ref, nb, k):
    return stat_ref[k : k + 1, :], stat_ref[nb + k : nb + k + 1, :]


def own_totals(e_ref, nb, amat, t_ref):
    t_ref[0:nb, :] = group_total(image_total(e_ref, 0, nb, amat))
    t_ref[nb : 2 * nb, :] = group_total(image_total(e_ref, nb, nb, amat))


def set_sums(e_ref, nb, k, x, y):
    e_ref[k : k + 1, :] = jnp.sum(x, axis=0, keepdims=True)
    e_ref[nb + k : nb + k + 1, :] = jnp.sum(y, axis=0, keepdims=True)


def silu(pre):
    return pre * jax.nn.sigmoid(pre)


def silu_slope(pre):
    s = jax.nn.sigmoid(pre)
    return s * (1.0 + pre * (1.0 - s))


def shift_columns(mid_ref, left_ref, right_ref, rows):
    left_ref[8 : 8 + rows, :] = mid_ref[7 : 7 + rows, :]
    right_ref[8 : 8 + rows, :] = mid_ref[9 : 9 + rows, :]


def make_patch(refs, patch_ref, mask_ref, ints_ref, k, chans):
    side = ints_ref[0, k]
    for dr in (-1, 0, 1):
        at = 8 + HALO + k * BLK
        if dr != 0:
            at = pl.multiple_of(at + dr * side, 8)
        for dc in (-1, 0, 1):
            tap = (dr + 1) * 3 + dc + 1
            rows = refs[dc + 1][pl.ds(at, BLK), :]
            if tap != 4:
                rows = rows * mask_ref[k * BLK : (k + 1) * BLK, tap : tap + 1]
            patch_ref[k * BLK : (k + 1) * BLK, tap * chans : (tap + 1) * chans] = rows.astype(bf16)


def lookup_kernel(tokens, *refs):
    index_ref, book_ref, out_ref = refs[tokens:]
    codes = book_ref.shape[0]
    total = jnp.zeros(out_ref.shape, f32)
    for c in range(0, codes, 512):
        lane = lax.broadcasted_iota(jnp.int32, (index_ref.shape[0], 512), 1) + c
        hot = jnp.where(index_ref[...] == lane, 1.0, 0.0).astype(bf16)
        total = total + dot_nn(hot, book_ref[c : c + 512, :])
    out_ref[...] = total.astype(bf16)


def lookup(index, book, tokens=()):
    pixels, emb = index.shape[0], book.shape[1]
    step = 512
    return pl.pallas_call(
        functools.partial(lookup_kernel, len(tokens)),
        grid=(pixels // step,),
        out_shape=sds((pixels, emb), bf16),
        in_specs=[HB] * len(tokens) + [pl.BlockSpec((step, 1), lambda i: (i, 0)), pl.BlockSpec(book.shape, lambda i: (0, 0))],
        out_specs=pl.BlockSpec((step, emb), lambda i: (i, 0)),
        compiler_params=pltpu.CompilerParams(vmem_limit_bytes=40 * MIB),
        cost_estimate=pl.CostEstimate(
            flops=2 * pixels * book.shape[0] * emb, bytes_accessed=book.size * 2, transcendentals=0
        ),
    )(*tokens, index, book)


def scatter_kernel(step, tokens, parts, *refs):
    index_refs, grad_refs = refs[tokens : tokens + parts], refs[tokens + parts : tokens + 3 * parts]
    begun_ref, out_ref = refs[-2:]
    half, emb = step * pl.num_programs(0), grad_refs[0].shape[1]
    for side in range(2):
        lanes = slice(side * emb, (side + 1) * emb)
        code = lax.broadcasted_iota(jnp.int32, (step, 512), 0) + (pl.program_id(0) * step + side * half)
        total = begun_ref[:, lanes]
        for index_ref, one_ref, two_ref in zip(index_refs, grad_refs[::2], grad_refs[1::2]):
            for p in range(0, one_ref.shape[0], 512):
                hot = jnp.where(index_ref[0:1, p : p + 512] == code, 1.0, 0.0).astype(bf16)
                grad = one_ref[p : p + 512, :].astype(f32) + two_ref[p : p + 512, :].astype(f32)
                total = total + dot_nn(hot, grad.astype(bf16))
        out_ref[:, lanes] = total.astype(out_ref.dtype)


def scatter(indices, pairs, codes, dtype, begun, tokens):
    grads = [x for pair in pairs for x in pair]
    emb, step, parts = grads[0].shape[1], 256, len(pairs)
    whole = [pl.BlockSpec(a.shape, lambda i: (0, 0)) for a in (*indices, *grads)]
    tile = pl.BlockSpec((step, 2 * emb), lambda i: (i, 0))
    return pl.pallas_call(
        functools.partial(scatter_kernel, step, len(tokens), parts),
        grid=(codes // 2 // step,),
        out_shape=sds((codes // 2, 2 * emb), dtype),
        in_specs=[HB for _ in tokens] + whole + [tile],
        out_specs=tile,
        compiler_params=pltpu.CompilerParams(vmem_limit_bytes=40 * MIB),
        cost_estimate=pl.CostEstimate(
            flops=2 * parts * grads[0].shape[0] * codes * emb, bytes_accessed=codes * emb * 8, transcendentals=0
        ),
    )(*tokens, *indices, *grads, begun)


def own_kernel(step, pass_ref, token_ref, index_ref, grad_ref, quant_ref, err_ref, in_ref, one_ref, two_ref, three_ref,
               query_ref, value_ref, proj_ref, passed_ref, out_ref, small_ref):
    emb = grad_ref.shape[1]
    half = out_ref.shape[0]
    for r in range(0, half, step):
        for side in range(2):
            code = lax.broadcasted_iota(jnp.int32, (step, 512), 0) + (r + side * half)
            total = jnp.zeros((step, emb), f32)
            for p in range(0, grad_ref.shape[0], 512):
                hot = jnp.where(index_ref[0:1, p : p + 512] == code, 1.0, 0.0).astype(bf16)
                total = total + dot_nn(hot, grad_ref[p : p + 512, :])
            out_ref[r : r + step, side * emb : (side + 1) * emb] = total
    small_ref[0:emb, :] = dot_tn(quant_ref[...], err_ref[...]).astype(bf16)
    rows = [in_ref[0:1, :], one_ref[0:3, :], two_ref[0:3, :], three_ref[0:2, :], query_ref[...], value_ref[...], proj_ref[...]]
    filler = jnp.zeros((small_ref.shape[0] - emb - 12, small_ref.shape[1]), f32)
    small_ref[emb:, :] = jnp.concatenate([*rows, filler], axis=0).astype(bf16)


def own_part(passed, token, index, grad, quant, err, vectors, codes):
    emb, chans = grad.shape[1], err.shape[1]
    outs = [(sds(passed.shape, bf16), HB), (sds((codes // 2, 2 * emb), f32), VM), (sds((chans, chans), bf16), VM)]
    operands = (passed, token, index, grad, quant, err, *vectors)
    flops = 2 * grad.shape[0] * emb * (codes + chans)
    return call(functools.partial(own_kernel, 256), [HB] * 2 + [VM] * (len(operands) - 2), outs, [], operands, flops, aliases={0: 0})


def lift_kernel(n_codes, nb, *refs):
    feat_ref, code_refs = refs[0], refs[1 : 1 + n_codes]
    w_ref, b_ref, amat_ref, quant_ref, resid_ref, t_ref, msgp_ref, msgn_ref, e_ref = refs[1 + n_codes :]
    pixels = feat_ref.shape[0]
    for c in range(0, pixels, CHUNK):
        at = slice(c, c + CHUNK)
        code = code_refs[0][at, :].astype(f32)
        for other in code_refs[1:]:
            code = code + other[at, :].astype(f32)
        quant = (feat_ref[at, :].astype(f32) + code).astype(bf16)
        quant_ref[at, :] = quant
        resid_ref[at, :] = dot_nn(quant, w_ref[...]) + b_ref[...]
    for k in range(nb):
        x = resid_ref[k * BLK : (k + 1) * BLK, :]
        set_sums(e_ref, nb, k, x, x * x)
    own_totals(e_ref, nb, amat_ref[...], t_ref)
    send_rows(resid_ref, t_ref, nb, msgp_ref, msgn_ref)


def send_rows(x_ref, t_ref, nb, msgp_ref, msgn_ref):
    pixels = x_ref.shape[0]
    msgp_ref[0:HALO, :] = x_ref[0:HALO, :]
    msgn_ref[0:HALO, :] = x_ref[pixels - HALO : pixels, :]
    send_stats(t_ref, nb, msgp_ref, msgn_ref, HALO)


def send_stats(t_ref, nb, msgp_ref, msgn_ref, at):
    msgp_ref[at : at + 8, :] = stat_rows(t_ref[0:1, :], t_ref[nb : nb + 1, :])
    msgn_ref[at : at + 8, :] = stat_rows(t_ref[nb - 1 : nb, :], t_ref[2 * nb - 1 : 2 * nb, :])


def get_stats(ref, at):
    return ref[at : at + 1, :], ref[at + 1 : at + 2, :]


def conv_forward_kernel(nb, last, *refs):
    x_ref, rp_ref, rn_ref, t_ref, amat_ref, gain_ref, bias_ref, mask_ref, ints_ref, w_hbm, cb_ref = refs[:11]
    refs = refs[11:]
    if last:
        resid_ref, cot_ref = refs[:2]
        refs = refs[2:]
    out_ref, stat_ref, to_ref, msgp_ref, msgn_ref, patch_hbm = refs[:6]
    mid_ref, left_ref, right_ref, patch_ref, w_ref, e_ref, w_sem, p_sem = refs[6:]
    pixels, chans = x_ref.shape
    load = pltpu.make_async_copy(w_hbm, w_ref, w_sem)
    load.start()
    amat = amat_ref[...]
    norm_stats(t_ref, nb, amat, get_stats(rp_ref, HALO), get_stats(rn_ref, HALO), stat_ref)
    gain, bias = gain_ref[...], bias_ref[...]

    def act(x, k):
        mean, inv = block_stats(stat_ref, nb, k)
        return silu((x - mean) * (inv * gain) + bias).astype(bf16).astype(f32)

    mid_ref[8 : 8 + HALO, :] = act(rp_ref[0:HALO, :], 0)
    mid_ref[8 + HALO + pixels : 8 + 2 * HALO + pixels, :] = act(rn_ref[0:HALO, :], nb - 1)
    for k in range(nb):
        mid_ref[8 + HALO + k * BLK : 8 + HALO + (k + 1) * BLK, :] = act(x_ref[k * BLK : (k + 1) * BLK, :], k)
    shift_columns(mid_ref, left_ref, right_ref, pixels + 2 * HALO)
    saves = []
    for c in range(0, pixels, CHUNK):
        for k in range(c // BLK, (c + CHUNK) // BLK):
            make_patch((left_ref, mid_ref, right_ref), patch_ref, mask_ref, ints_ref, k, chans)
        save = pltpu.make_async_copy(
            patch_ref.at[pl.ds(c, CHUNK), :], patch_hbm.at[pl.ds(c, CHUNK), :], p_sem.at[c // CHUNK]
        )
        save.start()
        saves.append(save)
        if c == 0:
            load.wait()
        out = dot_nn(patch_ref[c : c + CHUNK, :], w_ref[...]) + cb_ref[...]
        if last:
            out = out + resid_ref[c : c + CHUNK, :]
        out_ref[c : c + CHUNK, :] = out
        for k in range(c // BLK, (c + CHUNK) // BLK):
            x = out_ref[k * BLK : (k + 1) * BLK, :]
            set_sums(e_ref, nb, k, x, x * x)
    own_totals(e_ref, nb, amat, to_ref)
    if last:
        msgp_ref[0:pixels, :] = out_ref[...].astype(bf16)
        msgn_ref[0:pixels, :] = out_ref[...].astype(bf16)
        msgp_ref[pixels : pixels + HALO, :] = cot_ref[0:HALO, :]
        msgn_ref[pixels : pixels + HALO, :] = cot_ref[pixels - HALO : pixels, :]
        at = pixels + HALO
        msgp_ref[at : at + STAT, :] = pack_stats(to_ref[0:1, :], to_ref[nb : nb + 1, :])
        msgn_ref[at : at + STAT, :] = pack_stats(to_ref[nb - 1 : nb, :], to_ref[2 * nb - 1 : 2 * nb, :])
    else:
        send_rows(out_ref, to_ref, nb, msgp_ref, msgn_ref)
    for save in saves:
        save.wait()


def conv_scratch(pixels, chans, nb, w_shape):
    rows = pixels + 2 * HALO + 16
    return [
        pltpu.VMEM((rows, chans), f32),
        pltpu.VMEM((rows, chans), f32),
        pltpu.VMEM((rows, chans), f32),
        pltpu.VMEM((pixels, 9 * chans), bf16),
        pltpu.VMEM(w_shape, bf16),
        pltpu.VMEM((2 * nb, chans), f32),
    ]


def conv_forward(x, recv_p, recv_n, t, amat, gain, bias, mask, ints, weight, cb, resid=None, cot=None):
    pixels, chans = x.shape
    nb = pixels // BLK
    last = resid is not None
    msg = sds((pixels + HALO + STAT, chans), bf16) if last else sds((HALO + 8, chans), f32)
    operands = [x, recv_p, recv_n, t, amat, gain, bias, mask, ints, weight.reshape(9 * chans, chans), cb]
    ins = [VM, VM, VM, VM, VM, VM, VM, VM, SM, HB, VM]
    if last:
        operands += [resid, cot]
        ins += [VM, VM]
    stats = sds((2 * nb, chans), f32)
    outs = [(sds((pixels, chans), f32), VM), (stats, VM), (stats, VM), (msg, VM), (msg, VM)]
    outs.append((sds((pixels, 9 * chans), bf16), HB))
    scratch = conv_scratch(pixels, chans, nb, (9 * chans, chans))
    scratch += [pltpu.SemaphoreType.DMA, pltpu.SemaphoreType.DMA((pixels // CHUNK,))]
    flops = 18 * pixels * chans * chans
    return call(functools.partial(conv_forward_kernel, nb, last), ins, outs, scratch, operands, flops)


def attention_kernel(nb, *refs):
    (
        x_ref, rp_ref, rn_ref, t_ref, amat_ref, gain_ref, bias_ref, ints_ref, img_ref,
        wq_ref, wk_ref, wv_ref, wp_ref, bq_ref, bv_ref, bp_ref, cot_ref,
    ) = refs[:17]
    (
        norm_hbm, dk_hbm, dv_hbm, out_ref, attn_ref, dq_ref, u_ref, stat_ref, to_ref, vec_ref, msgp_ref, msgn_ref,
    ) = refs[17:29]
    norm_ref, dk_ref, dv_ref, q_ref, k_ref, v_ref, da_ref, at_ref, dqf_ref, dkf_ref, dvf_ref, e_ref, h_ref, sems = refs[29:]
    pixels, chans = x_ref.shape
    own = pixels // CHUNK
    scale = 1.0 / math.sqrt(chans)
    amat = amat_ref[...]
    at = pixels + HALO
    prev_stats = unpack_stats(rp_ref[at : at + STAT, :])
    next_stats = unpack_stats(rn_ref[at : at + STAT, :])
    norm_stats(t_ref, nb, amat, prev_stats, next_stats, stat_ref)
    gain, bias = gain_ref[...], bias_ref[...]
    chunk_lo = ints_ref[1, 0] // CHUNK
    chunk_hi = (ints_ref[2, nb - 1] + CHUNK - 1) // CHUNK
    copies = []

    def send(scratch, hbm, which, c):
        r = pl.ds(c * CHUNK, CHUNK)
        copy = pltpu.make_async_copy(scratch.at[r, :], hbm.at[r, :], sems.at[which, c])
        copy.start()
        copies.append(copy)

    def xhat(c, b):
        r = (c % own) * CHUNK + b * BLK
        if c < own:
            x, k = rp_ref[r : r + BLK, :].astype(f32), 0
        elif c < 2 * own:
            x, k = x_ref[r : r + BLK, :], r // BLK
        else:
            x, k = rn_ref[r : r + BLK, :].astype(f32), nb - 1
        mean, inv = block_stats(stat_ref, nb, k)
        return (x - mean) * inv

    def reached(c, work, otherwise):
        if own <= c < 2 * own:
            work()
        else:
            inside = (c >= chunk_lo) & (c < chunk_hi)
            pl.when(inside)(work)
            pl.when(jnp.logical_not(inside))(otherwise)

    for c in range(3 * own):
        r = slice(c * CHUNK, (c + 1) * CHUNK)

        def keys(c=c, r=r):
            for b in range(CHUNK // BLK):
                norm_ref[c * CHUNK + b * BLK : c * CHUNK + (b + 1) * BLK, :] = (xhat(c, b) * gain + bias).astype(bf16)
            normed = norm_ref[r, :]
            k_ref[r, :] = dot_nn(normed, wk_ref[...]).astype(bf16)
            v_ref[r, :] = (dot_nn(normed, wv_ref[...]) + bv_ref[...]).astype(bf16)
            dkf_ref[r, :] = jnp.zeros((CHUNK, chans), f32)
            dvf_ref[r, :] = jnp.zeros((CHUNK, chans), f32)
            if own <= c < 2 * own:
                o = slice((c - own) * CHUNK, (c - own + 1) * CHUNK)
                q_ref[o, :] = (dot_nn(normed, wq_ref[...]) + bq_ref[...]).astype(bf16)
                da_ref[o, :] = dot_nt(cot_ref[o, :], wp_ref[...]).astype(bf16)

        def nothing(r=r):
            norm_ref[r, :] = jnp.zeros((CHUNK, chans), bf16)

        reached(c, keys, nothing)
        send(norm_ref, norm_hbm, 0, c)
    q_ref[pixels : pixels + CHUNK, :] = jnp.zeros((CHUNK, chans), bf16)
    da_ref[pixels : pixels + CHUNK, :] = jnp.zeros((CHUNK, chans), bf16)

    def attend(count, key_at, row_at, row_end):
        rows = pl.ds(pl.multiple_of(row_at, BLK), CHUNK)
        cols = pl.ds(pl.multiple_of(key_at, BLK), count)
        s = dot_nt(q_ref[rows, :], k_ref[cols, :]) * scale
        p = jnp.exp(s - jnp.max(s, axis=1, keepdims=True))
        at_row = lax.broadcasted_iota(jnp.int32, (CHUNK, 1), 0) + row_at
        p = p * jnp.where(at_row < row_end, 1.0 / jnp.sum(p, axis=1, keepdims=True), 0.0)
        low = p.astype(bf16)
        d_attn = da_ref[rows, :]
        dp = dot_nt(d_attn, v_ref[cols, :])
        at_ref[rows, :] = dot_nn(low, v_ref[cols, :]).astype(bf16)
        dvf_ref[cols, :] += dot_tn(low, d_attn)
        ds = (p * (dp - jnp.sum(p * dp, axis=1, keepdims=True))).astype(bf16)
        dqf_ref[rows, :] = (dot_nn(ds, k_ref[cols, :]) * scale).astype(bf16)
        dkf_ref[cols, :] += dot_tn(ds, q_ref[rows, :])

    def image(m, carry):
        key_at, side, begin, end = (img_ref[t, m] for t in range(4))
        for kind in (GRID // 2, 3 * GRID // 4, GRID):

            @pl.when(side == kind)
            def _():
                def block(i, inner):
                    attend(kind * kind, key_at, begin + i * CHUNK, end)
                    return inner

                lax.fori_loop(0, (end - begin + CHUNK - 1) // CHUNK, block, 0)

        return carry

    lax.fori_loop(0, img_ref[4, 0], image, 0)
    h_ref[...] = jnp.zeros(h_ref.shape, f32)
    for c in range(3 * own):
        r = slice(c * CHUNK, (c + 1) * CHUNK)
        o = slice((c % own) * CHUNK, (c % own + 1) * CHUNK)

        def fold(c=c, r=r, o=o):
            d_key = (dkf_ref[r, :] * scale).astype(bf16)
            d_value = dvf_ref[r, :].astype(bf16)
            dk_ref[r, :] = d_key
            dv_ref[r, :] = d_value
            u = dot_nt(d_key, wk_ref[...]) + dot_nt(d_value, wv_ref[...])
            if own <= c < 2 * own:
                d_query = dqf_ref[o, :]
                dq_ref[o, :] = d_query
                attn = at_ref[o, :]
                attn_ref[o, :] = attn
                out_ref[o, :] = (x_ref[o, :] + dot_nn(attn, wp_ref[...]) + bp_ref[...]).astype(bf16)
                u_ref[o, :] = u + dot_nt(d_query, wq_ref[...])
                for b in range(CHUNK // BLK):
                    k = (c - own) * (CHUNK // BLK) + b
                    u = u_ref[k * BLK : (k + 1) * BLK, :]
                    set_sums(e_ref, nb, k, u, u * xhat(c, b))
            else:
                msg_ref, row = (msgp_ref, 0) if c < own else (msgn_ref, 2)
                msg_ref[o, :] = u.astype(bf16)
                for b in range(CHUNK // BLK):
                    part = u[b * BLK : (b + 1) * BLK, :]
                    h_ref[row : row + 1, :] += jnp.sum(part, axis=0, keepdims=True)
                    h_ref[row + 1 : row + 2, :] += jnp.sum(part * xhat(c, b), axis=0, keepdims=True)

        def nothing(c=c, r=r, o=o):
            zero = jnp.zeros((CHUNK, chans), bf16)
            dk_ref[r, :] = zero
            dv_ref[r, :] = zero
            (msgp_ref if c < own else msgn_ref)[o, :] = zero

        reached(c, fold, nothing)
        send(dk_ref, dk_hbm, 1, c)
        send(dv_ref, dv_hbm, 2, c)
    before, before_x, after, after_x = (h_ref[i : i + 1, :] for i in range(4))
    d_bias = jnp.sum(e_ref[0:nb, :], axis=0, keepdims=True) + before + after
    d_gain = jnp.sum(e_ref[nb : 2 * nb, :], axis=0, keepdims=True) + before_x + after_x
    vec_ref[...] = stat_rows(d_gain, d_bias)
    e_ref[0:1, :] += before
    e_ref[nb : nb + 1, :] += before_x
    e_ref[nb - 1 : nb, :] += after
    e_ref[2 * nb - 1 : 2 * nb, :] += after_x
    e_ref[...] = e_ref[...] * gain
    own_totals(e_ref, nb, amat, to_ref)
    msgp_ref[pixels : pixels + HALO, :] = u_ref[0:HALO, :].astype(bf16)
    msgn_ref[pixels : pixels + HALO, :] = u_ref[pixels - HALO : pixels, :].astype(bf16)
    msgp_ref[at : at + STAT, :] = pack_stats(to_ref[0:1, :], to_ref[nb : nb + 1, :])
    msgn_ref[at : at + STAT, :] = pack_stats(to_ref[nb - 1 : nb, :], to_ref[2 * nb - 1 : 2 * nb, :])
    for copy in copies:
        copy.wait()


def attention(x, recv_p, recv_n, t, amat, gain, bias, ints, images, wq, wk, wv, wp, bq, bv, bp, cot):
    pixels, chans = x.shape
    nb, ext = pixels // BLK, 3 * pixels
    rows16, rows32 = sds((pixels, chans), bf16), sds((pixels, chans), f32)
    ext16 = sds((ext, chans), bf16)
    stats = sds((2 * nb, chans), f32)
    msg = sds((pixels + HALO + STAT, chans), bf16)
    outs = [(ext16, HB)] * 3
    outs += [(o, VM) for o in (rows16, rows16, rows16, rows32, stats, stats, sds((8, chans), f32), msg, msg)]
    padded = pltpu.VMEM((pixels + CHUNK, chans), bf16)
    window = pltpu.VMEM((ext, chans), bf16)
    wide = pltpu.VMEM((ext, chans), f32)
    scratch = [window, window, window, padded, window, window, padded, padded, padded, wide, wide]
    scratch += [pltpu.VMEM((2 * nb, chans), f32), pltpu.VMEM((8, chans), f32)]
    scratch.append(pltpu.SemaphoreType.DMA((3, ext // CHUNK)))
    ins = [VM] * 7 + [SM, SM] + [VM] * 8
    operands = (x, recv_p, recv_n, t, amat, gain, bias, ints, images, wq, wk, wv, wp, bq, bv, bp, cot)
    flops = 2 * pixels * chans * (chans * 9 + 6 * 1280)
    return call(functools.partial(attention_kernel, nb), ins, outs, scratch, operands, flops)


def conv_backward_kernel(nb, first, *refs):
    refs = refs[1:]
    if first:
        u_ref, mine_p_ref, mine_n_ref, rp_ref, rn_ref, xp_ref, xn_ref, cot_ref = refs[:8]
        refs = refs[8:]
    else:
        u_ref, rp_ref, rn_ref, xp_ref, xn_ref = refs[:5]
        refs = refs[5:]
    x_ref, stat_ref, s_ref, gain_ref, amat_ref, mask_ref, ints_ref, w_hbm = refs[:8]
    y_ref, ystat_ref, ygain_ref, ybias_ref = refs[8:12]
    refs = refs[12:]
    if first:
        mid_out_ref, refs = refs[0], refs[1:]
    err_ref, v_ref, so_ref, vec_ref, msgp_ref, msgn_ref = refs[:6]
    mid_ref, left_ref, right_ref, patch_ref, w_ref, e_ref, w_sem = refs[6:]
    pixels, chans = x_ref.shape
    loads = []
    for tap in range(9):
        load = pltpu.make_async_copy(
            w_hbm.at[8 - tap], w_ref.at[:, pl.ds(tap * chans, chans)], w_sem.at[tap]
        )
        load.start()
        loads.append(load)
    amat = amat_ref[...]
    if first:
        at = pixels + HALO
        prev_stats = unpack_stats(rp_ref[at : at + STAT, :])
        next_stats = unpack_stats(rn_ref[at : at + STAT, :])
    else:
        prev_stats, next_stats = get_stats(rp_ref, HALO), get_stats(rn_ref, HALO)
    one, two = totals(s_ref, nb, amat, prev_stats, next_stats)
    e_ref[0:nb, :] = one
    e_ref[nb : 2 * nb, :] = two
    gain = gain_ref[...]

    def grad(u, x, k):
        mean, inv = block_stats(stat_ref, nb, k)
        m_one, m_two = block_stats(e_ref, nb, k)
        return inv * (u * gain - m_one - (x - mean) * inv * m_two)

    if first:
        low, high = slice(pixels - HALO, pixels), slice(0, HALO)
        side = slice(pixels, pixels + HALO)
        u = mine_p_ref[low, :].astype(f32) + rp_ref[side, :].astype(f32)
        before = xp_ref[side, :].astype(f32) + grad(u, xp_ref[low, :].astype(f32), 0)
        u = mine_n_ref[high, :].astype(f32) + rn_ref[side, :].astype(f32)
        after = xn_ref[side, :].astype(f32) + grad(u, xn_ref[high, :].astype(f32), nb - 1)
    else:
        before = grad(rp_ref[0:HALO, :], xp_ref[0:HALO, :], 0)
        after = grad(rn_ref[0:HALO, :], xn_ref[0:HALO, :], nb - 1)
    mid_ref[8 : 8 + HALO, :] = before.astype(bf16).astype(f32)
    mid_ref[8 + HALO + pixels : 8 + 2 * HALO + pixels, :] = after.astype(bf16).astype(f32)
    column = jnp.zeros((1, chans), f32)
    for k in range(nb):
        r = slice(k * BLK, (k + 1) * BLK)
        u = u_ref[r, :]
        if first:
            u = u + rp_ref[r, :].astype(f32) + rn_ref[r, :].astype(f32)
        g = grad(u, x_ref[r, :], k)
        if first:
            g = g + cot_ref[r, :].astype(f32)
            mid_out_ref[r, :] = g
        low = g.astype(bf16)
        err_ref[r, :] = low
        g = low.astype(f32)
        column = column + jnp.sum(g, axis=0, keepdims=True)
        mid_ref[8 + HALO + k * BLK : 8 + HALO + (k + 1) * BLK, :] = g
    shift_columns(mid_ref, left_ref, right_ref, pixels + 2 * HALO)
    y_gain, y_bias = ygain_ref[...], ybias_ref[...]
    for c in range(0, pixels, CHUNK):
        for k in range(c // BLK, (c + CHUNK) // BLK):
            make_patch((left_ref, mid_ref, right_ref), patch_ref, mask_ref, ints_ref, k, chans)
        if c == 0:
            for load in loads:
                load.wait()
        v_ref[c : c + CHUNK, :] = dot_nt(patch_ref[c : c + CHUNK, :], w_ref[...])
        for k in range(c // BLK, (c + CHUNK) // BLK):
            r = slice(k * BLK, (k + 1) * BLK)
            mean, inv = block_stats(ystat_ref, nb, k)
            xh = (y_ref[r, :] - mean) * inv
            v = v_ref[r, :] * silu_slope(xh * y_gain + y_bias)
            v_ref[r, :] = v
            set_sums(e_ref, nb, k, v, v * xh)
    d_bias = jnp.sum(e_ref[0:nb, :], axis=0, keepdims=True)
    d_gain = jnp.sum(e_ref[nb : 2 * nb, :], axis=0, keepdims=True)
    vec_ref[...] = jnp.concatenate([d_gain, d_bias, column, jnp.zeros((5, chans), f32)], axis=0)
    e_ref[...] = e_ref[...] * y_gain
    own_totals(e_ref, nb, amat, so_ref)
    if first:
        send_rows(v_ref, so_ref, nb, msgp_ref, msgn_ref)
    else:
        send_stats(so_ref, nb, msgp_ref, msgn_ref, 0)


def conv_backward(first, token, heads, x, stat, s, gain, amat, mask, ints, weight, y, ystat, ygain, ybias):
    pixels, chans = x.shape
    nb = pixels // BLK
    operands = [token, *heads, x, stat, s, gain, amat, mask, ints, weight.reshape(9, chans, chans), y, ystat, ygain, ybias]
    ins = [HB] + [VM] * len(heads) + [VM] * 6 + [SM, HB] + [VM] * 4
    msg = sds((HALO + 8 if first else 8, chans), f32)
    rows = sds((pixels, chans), f32)
    outs = [rows] if first else []
    outs += [sds((pixels, chans), bf16), rows, sds((2 * nb, chans), f32), sds((8, chans), f32), msg, msg]
    scratch = conv_scratch(pixels, chans, nb, (chans, 9 * chans)) + [pltpu.SemaphoreType.DMA((9,))]
    flops = 18 * pixels * chans * chans
    return call(
        functools.partial(conv_backward_kernel, nb, first), ins, [(o, VM) for o in outs], scratch, operands, flops
    )


def tail_kernel(nb, passes, *refs):
    v_ref, rp_ref, rn_ref, s_ref, x_ref, stat_ref, gain_ref, amat_ref, mid_ref, w_ref = refs[passes : passes + 10]
    err_ref, fg_ref, vec_ref, e_ref = refs[2 * passes + 10 :]
    pixels, chans = x_ref.shape
    one, two = totals(s_ref, nb, amat_ref[...], get_stats(rp_ref, 0), get_stats(rn_ref, 0))
    e_ref[0:nb, :] = one
    e_ref[nb : 2 * nb, :] = two
    gain = gain_ref[...]
    column = jnp.zeros((1, chans), f32)
    for c in range(0, pixels, CHUNK):
        for k in range(c // BLK, (c + CHUNK) // BLK):
            r = slice(k * BLK, (k + 1) * BLK)
            mean, inv = block_stats(stat_ref, nb, k)
            m_one, m_two = block_stats(e_ref, nb, k)
            g = mid_ref[r, :] + inv * (v_ref[r, :] * gain - m_one - (x_ref[r, :] - mean) * inv * m_two)
            low = g.astype(bf16)
            err_ref[r, :] = low
            column = column + jnp.sum(low.astype(f32), axis=0, keepdims=True)
        fg_ref[c : c + CHUNK, :] = dot_nt(err_ref[c : c + CHUNK, :], w_ref[...]).astype(bf16)
    vec_ref[...] = jnp.concatenate([column, jnp.zeros((7, chans), f32)], axis=0)


def tail(passed, v, recv_p, recv_n, s, x, stat, gain, amat, mid, w_in):
    pixels, chans = x.shape
    nb = pixels // BLK
    count = len(passed)
    outs = [(sds(a.shape, a.dtype), HB) for a in passed]
    outs += [(sds((pixels, chans), bf16), VM), (sds((pixels, w_in.shape[0]), bf16), VM), (sds((8, chans), f32), VM)]
    operands = (*passed, v, recv_p, recv_n, s, x, stat, gain, amat, mid, w_in)
    scratch = [pltpu.VMEM((2 * nb, chans), f32)]
    flops = 2 * pixels * chans * w_in.shape[0]
    body = functools.partial(tail_kernel, nb, count)
    aliases = {i: i for i in range(count)}
    return call(body, [HB] * count + [VM] * 10, outs, scratch, operands, flops, aliases=aliases)


def finish_kernel(places, tokens, *refs):
    up_ref, mine_hbm, other_hbm, *out_refs, read_ref, stage_ref, read_sems, sems = refs[tokens:]
    slots = stage_ref.shape[0]

    def write(own):
        work = []
        for source, half in ((mine_hbm, own), (other_hbm, 1 - own)):
            for row, moves in places(half, out_refs):
                work.append((source.at[pl.ds(row, CHUNK), :], moves))
        reads = [
            pltpu.make_async_copy(source, read_ref.at[i % slots], read_sems.at[i % slots])
            for i, (source, _) in enumerate(work)
        ]
        for read in reads[:slots]:
            read.start()
        pending = [[] for _ in range(slots)]
        for i, (_, moves) in enumerate(work):
            slot = i % slots
            reads[i].wait()
            for copy in pending[slot]:
                copy.wait()
            stage_ref[slot] = read_ref[slot].astype(f32)
            if i + slots < len(work):
                reads[i + slots].start()
            pending[slot] = []
            for k, (lanes, target) in enumerate(moves):
                copy = pltpu.make_async_copy(stage_ref.at[slot, :, lanes], target, sems.at[slot, k])
                copy.start()
                pending[slot].append(copy)
        for copies in pending:
            for copy in copies:
                copy.wait()

    for own in range(2):
        pl.when(up_ref[0] == own)(functools.partial(write, own))


def finish(places, up, mine, outs, tokens=()):
    chans = mine.shape[1]
    slots = 16
    scratch = [pltpu.VMEM((slots, CHUNK, chans), bf16), pltpu.VMEM((slots, CHUNK, chans), f32)]
    scratch += [pltpu.SemaphoreType.DMA((slots,)), pltpu.SemaphoreType.DMA((slots, 2))]
    body = functools.partial(finish_kernel, places, len(tokens))
    operands = (*tokens, up.reshape(1), mine, partner(mine, "rows", 1))
    return call(body, [HB] * len(tokens) + [SM, HB, HB], [(o, HB) for o in outs], scratch, operands, 0)


def conv_places(half, out_ref):
    rows = out_ref.shape[0] // 2
    return [(r, [(slice(None), out_ref.at[pl.ds(half * rows + r, CHUNK), :])]) for r in range(0, rows, CHUNK)]


def early_places(half, out_refs):
    conv_ref, *squares = out_refs
    out = conv_places(half, conv_ref)
    row = conv_ref.shape[0] // 2
    for ref in squares[2 * half : 2 * half + 2]:
        for r in range(0, ref.shape[0], CHUNK):
            out.append((row, [(slice(None), ref.at[pl.ds(r, CHUNK), :])]))
            row += CHUNK
    return out


def late_places(half, out_refs):
    conv_ref, in_ref, vec_ref = out_refs
    return conv_places(half, conv_ref) + [(conv_ref.shape[0] // 2, [(slice(None), (in_ref, vec_ref)[half])])]


def book_places(half, out_refs):
    (book_ref,) = out_refs
    quarter, emb = book_ref.shape[0] // 4, book_ref.shape[1]
    out = []
    for r in range(0, quarter, CHUNK):
        to = half * quarter + r
        left = (pl.ds(0, emb), book_ref.at[pl.ds(to, CHUNK), :])
        right = (pl.ds(emb, emb), book_ref.at[pl.ds(2 * quarter + to, CHUNK), :])
        out.append((r, [left, right]))
    return out


def gate_kernel(*refs):
    pass


def gate(passed, *tokens):
    outs = [(sds(passed.shape, passed.dtype), HB)]
    return call(gate_kernel, [HB] * (1 + len(tokens)), outs, [], (passed, *tokens), 0, aliases={0: 0}, light=True)[0]


def along(array, axis, by):
    count = lax.axis_size(axis)
    return lax.ppermute(array, axis, [(i, i + by) for i in range(count) if 0 <= i + by < count])


def around(array, axis, by):
    count = lax.axis_size(axis)
    return lax.ppermute(array, axis, [(i, (i + by) % count) for i in range(count)])


def swap(to_prev, to_next):
    return along(to_next, "rows", 1), along(to_prev, "rows", -1)


def partner(array, axis, bit):
    return lax.ppermute(array, axis, [(i, i ^ bit) for i in range(lax.axis_size(axis))])


def bits(axis):
    return [(axis, 1 << b) for b in range(lax.axis_size(axis).bit_length() - 1)]


def half_of(x, which):
    return lax.dynamic_slice_in_dim(x, which * (x.shape[0] // 2), x.shape[0] // 2)


def core_send(arrays):
    up = lax.axis_index("rows") % 2
    send = [half_of(x, 1 - up) for x in arrays]
    return partner(jnp.concatenate(send) if len(send) > 1 else send[0], "rows", 1)


def add(one, two):
    return (one.astype(f32) + two.astype(f32)).astype(bf16)


def join(parts):
    return jnp.concatenate(parts) if len(parts) > 1 else parts[0]


def exchange(axis, bit, jobs):
    up = (lax.axis_index(axis) // bit) % 2
    keep = [half_of(x, up) if reduce else x for reduce, x in jobs]
    got = partner(join([half_of(x, 1 - up) if reduce else x for reduce, x in jobs]), axis, bit)
    at, out = 0, []
    for (reduce, _), x in zip(jobs, keep):
        other = got[at : at + x.shape[0]]
        at += x.shape[0]
        if reduce:
            out.append(add(x, other))
        else:
            out.append(jnp.where(up == 0, jnp.concatenate([x, other]), jnp.concatenate([other, x])))
    return out


def plan(flip, *axes):
    middle = bits(axes[0])[1:]
    steps = (middle[::-1] if flip else middle) + [step for axis in axes[1:] for step in bits(axis)]
    return [(step, True) for step in steps] + [(step, False) for step in steps[::-1]]


def rounds(arrays, plans, begins, turns=None):
    arrays = list(arrays)
    for turn in turns or range(max(begin + len(p) for p, begin in zip(plans, begins))):
        by_partner = {}
        for i, (p, begin) in enumerate(zip(plans, begins)):
            if 0 <= turn - begin < len(p):
                step, reduce = p[turn - begin]
                by_partner.setdefault((begin, *step), []).append((i, reduce))
        for (_, *step), jobs in by_partner.items():
            out = exchange(*step, [(reduce, arrays[i]) for i, reduce in jobs])
            for (i, _), x in zip(jobs, out):
                arrays[i] = x
    return arrays


def streams(x, *axes):
    world = math.prod(lax.axis_size(axis) for axis in axes) // 2
    unit = 16 * world
    cut = -(-x.shape[0] // (2 * unit)) * unit
    return [x[:cut], x[cut:]]


def half_of(x, which):
    return lax.dynamic_slice_in_dim(x, which * (x.shape[0] // 2), x.shape[0] // 2)


def core_send(x):
    return partner(half_of(x, 1 - lax.axis_index("rows") % 2), "rows", 1)


def core_half(x):
    return half_of(x, lax.axis_index("rows") % 2)


def core_swap(x):
    return core_half(x), core_send(x)


def per_device(
    features, indices, img_width, img_start, codebook, w_in, b_in, gn1_gain, gn1_bias, conv1_w, conv1_b,
    gn2_gain, gn2_bias, conv2_w, conv2_b, gn3_gain, gn3_bias, w_query, b_query, w_key, w_value, b_value,
    w_proj, b_proj, cotangent,
):
    pixels, emb = features.shape[1], features.shape[2]
    chans = w_in.shape[1]
    nb = pixels // BLK
    widths, starts = img_width[0], img_start[0]
    first_pos = lax.axis_index("rows") * pixels
    row = lambda v: v.reshape(1, -1)

    positions = first_pos + jnp.arange(pixels, dtype=jnp.int32)
    image_id = jnp.sum((starts[None, :] <= positions[:, None]).astype(jnp.int32), axis=1) - 1
    choose = image_id[:, None] == jnp.arange(widths.shape[0], dtype=jnp.int32)[None, :]
    side = jnp.sum(jnp.where(choose, widths[None, :], 0), axis=1)
    begin = jnp.sum(jnp.where(choose, starts[None, :], 0), axis=1)
    offset = positions - begin
    safe = jnp.maximum(side, 1)
    row_at, col_at = offset // safe, offset % safe
    valid = []
    for dr in (-1, 0, 1):
        for dc in (-1, 0, 1):
            r, c = row_at + dr, col_at + dc
            valid.append((r >= 0) & (r < side) & (c >= 0) & (c < side))
    mask = jnp.stack(valid, axis=1).astype(f32)
    low_key = begin - first_pos + pixels
    spans = jnp.stack([low_key, low_key + side * side], axis=1)
    block_id = image_id[::BLK]
    ints = jnp.stack([side[::BLK], spans[::BLK, 0], spans[::BLK, 1]])
    count = (jnp.maximum(side * side, 1)[::BLK] * (chans // GN_GROUPS)).astype(f32)
    amat = jnp.concatenate(
        [
            (block_id[:, None] == block_id[None, :]).astype(f32),
            (block_id == block_id[0]).astype(f32)[:, None],
            (block_id == block_id[-1]).astype(f32)[:, None],
            (1.0 / count)[:, None],
        ],
        axis=1,
    )

    at_image = jnp.minimum(block_id[0] + jnp.arange(8, dtype=jnp.int32), widths.shape[0] - 1)
    pick = at_image[:, None] == jnp.arange(widths.shape[0], dtype=jnp.int32)[None, :]
    img_side = jnp.sum(jnp.where(pick, widths[None, :], 0), axis=1)
    img_at = jnp.sum(jnp.where(pick, starts[None, :], 0), axis=1) - first_pos
    images = jnp.stack(
        [
            img_at + pixels,
            img_side,
            jnp.maximum(img_at, 0),
            jnp.minimum(img_at + img_side * img_side, pixels),
            jnp.broadcast_to(block_id[-1] - block_id[0] + 1, (8,)),
        ]
    )

    groups = lax.axis_size("chan")
    codes = codebook.shape[0]
    ring = [indices[0]] + [around(indices, "chan", -d)[0] for d in range(1, groups)]
    local = [index - lax.axis_index("chan") * codes for index in ring]
    found = [lookup(index[:, None], codebook) for index in local[1:]]
    found.insert(0, lookup(local[0][:, None], codebook, found))
    rows_in = [found[0]] + [around(found[d], "chan", d) for d in range(1, groups)]

    stats2 = sds((2 * nb, chans), f32)
    rows32 = sds((pixels, chans), f32)
    msg32 = sds((HALO + 8, chans), f32)
    quant, resid_in, t_one, to_p, to_n = call(
        functools.partial(lift_kernel, groups, nb),
        [VM] * (4 + groups),
        [(o, VM) for o in (sds((pixels, emb), bf16), rows32, stats2, msg32, msg32)],
        [pltpu.VMEM((2 * nb, chans), f32)],
        (features[0], *rows_in, w_in, row(b_in), amat),
        2 * pixels * emb * chans,
    )
    p_one, n_one = swap(to_p, to_n)
    hid_one, stat_one, t_two, to_p, to_n, patch_one = conv_forward(
        resid_in, p_one, n_one, t_one, amat, row(gn1_gain), row(gn1_bias), mask, ints, conv1_w, row(conv1_b)
    )
    p_two, n_two = swap(to_p, to_n)
    cot = cotangent[0]
    resid_mid, stat_two, t_three, to_p, to_n, patch_two = conv_forward(
        hid_one, p_two, n_two, t_two, amat, row(gn2_gain), row(gn2_bias), mask, ints, conv2_w, row(conv2_b),
        resid_in, cot,
    )
    p_three, n_three = swap(to_p, to_n)
    normed, d_key, d_value, output, attn, d_query, u_own, stat_three, s_three, vec_three, to_p, to_n = attention(
        resid_mid, p_three, n_three, t_three, amat, row(gn3_gain), row(gn3_bias), ints, images,
        w_query, w_key, w_value, w_proj, row(b_query), row(b_value), row(b_proj), cot,
    )
    p_back, n_back = swap(to_p, to_n)
    tn = lambda a, b: jnp.einsum("nk,nc->kc", a, b, preferred_element_type=f32).astype(bf16)
    own_normed = normed[pixels : 2 * pixels]
    g_proj = tn(attn, cot)
    g_query = tn(own_normed, d_query)
    g_key = tn(normed, d_key)
    g_value = tn(normed, d_value)
    g_attn = jnp.concatenate([g_proj, g_query, g_key, g_value])
    g_b_proj = jnp.sum(cot.astype(f32), axis=0, keepdims=True)
    g_b_query = jnp.sum(d_query.astype(f32), axis=0, keepdims=True)
    g_b_value = jnp.sum(d_value.astype(f32), axis=0, keepdims=True)
    d_mid, err_two, v_two, s_two, vec_two, msg_p, msg_n = conv_backward(
        True, g_attn, (u_own, to_p, to_n, p_back, n_back, p_three, n_three, cot),
        resid_mid, stat_three, s_three, row(gn3_gain), amat, mask, ints, conv2_w,
        hid_one, stat_two, row(gn2_gain), row(gn2_bias),
    )
    p_four, n_four = swap(msg_p, msg_n)
    g_conv2 = tn(patch_two, err_two)
    two_got, attn_got = core_send(g_conv2), core_send(g_attn)
    err_one, v_one, s_one, vec_one, msg_p, msg_n = conv_backward(
        False, g_conv2, (v_two, p_four, n_four, p_two, n_two),
        hid_one, stat_two, s_two, row(gn2_gain), amat, mask, ints, conv1_w,
        resid_in, stat_one, row(gn1_gain), row(gn1_bias),
    )
    p_five, n_five = swap(msg_p, msg_n)
    err_one, two_got, attn_got, err_in, feature_grad, vec_in = tail(
        (err_one, two_got, attn_got), v_one, p_five, n_five, s_one, resid_in, stat_one, row(gn1_gain), amat, d_mid, w_in
    )
    below, above = [feature_grad], [feature_grad]
    for _ in range(1, groups):
        below.append(along(below[-1], "chan", 1))
        above.append(along(above[-1], "chan", -1))
    two = jnp.concatenate([add(core_half(g_conv2), two_got), add(core_half(g_attn), attn_got)])
    g_conv1 = tn(patch_one, gate(err_one, two))
    vectors = (vec_in, vec_one, vec_two, vec_three, g_b_query, g_b_value, g_b_proj)
    both = [plan(flip, "rows", "chan") for flip in (False, True)]
    plans = both + both + both[1:] + [plan(flip, "rows") for flip in (False, True)]
    begins = [0, 0, LATE_ROUND, LATE_ROUND, LATE_ROUND, BOOK_ROUND, BOOK_ROUND]
    work = rounds(streams(two, "rows", "chan"), plans[:2], begins, range(1))
    g_conv1, begun, small = own_part(g_conv1, work[0], row(local[0]), feature_grad, quant, err_in, vectors, codes)
    one = add(*core_swap(g_conv1))
    small = add(*core_swap(small))
    pair = lambda d: (row(local[groups - d]), (below[d], above[groups - d]))
    middle = [pair(d) for d in range(1, groups) if 2 * d == groups]
    outer = [pair(d) for d in range(1, groups) if 2 * d != groups]
    book = scatter(*zip(*middle), codes, f32, begun, work)
    work = rounds(work, plans[:2], begins, range(1, 2))
    book = scatter(*zip(*outer), codes, bf16, book, work)
    book = add(*core_swap(book))
    work += streams(one, "rows", "chan") + [small] + streams(book, "rows")
    turns = max(begin + len(p) for p, begin in zip(plans, begins))
    work = rounds(work, plans, begins, range(2, turns))
    up = lax.axis_index("rows") % 2
    square, conv = sds((chans, chans), f32), sds((9 * chans, chans), f32)
    early = finish(early_places, up, jnp.concatenate(work[:2]), [conv] + [square] * 4)
    book = finish(book_places, up, jnp.concatenate(work[5:]), [sds((codes, emb), f32)])
    narrow = [sds((emb, chans), f32), sds((chans - emb, chans), f32)]
    sum_one, s_in, vec = finish(
        late_places, up, jnp.concatenate(work[2:5]), [conv] + narrow, (early[0], book[0])
    )
    sum_two, s_proj, s_query, s_key, s_value = early
    (book_grad,) = book
    return (
        output[None],
        feature_grad[None],
        book_grad,
        s_in,
        vec[0],
        vec[1],
        vec[2],
        sum_one.reshape(conv1_w.shape),
        vec[3],
        vec[4],
        vec[5],
        sum_two.reshape(conv2_w.shape),
        vec[6],
        vec[7],
        vec[8],
        s_query,
        vec[9],
        s_key,
        s_value,
        vec[10],
        s_proj,
        vec[11],
    )


def solution(mesh):
    group, copied = P("chan", "rows", None), P()
    placed = (group, P("chan", "rows"), P("chan", None), P("chan", None), P("chan", None))
    return jax.shard_map(
        per_device,
        mesh=mesh,
        in_specs=placed + (copied,) * 19 + (group,),
        out_specs=(group, group, P("chan", None)) + (copied,) * 19,
        check_vma=False,
    )
```
